32 devices in a mesh: tx: 4 (over x, core), ty: 8 (over z, y).
Axes of the slice: x: 2, y: 2, z: 4, core: 2. Of those that a mesh axis runs over, the one named last changes fastest.
Arguments:
- signal: float32 [8388608], P(('tx', 'ty')), may hold values from -6 to 6
- band_start: int32 [64], replicated, may hold values from 0 to 8372192
- band_width: int32 [64], replicated, may hold values from 2048 to 16384, as said below
- band_gain: float32 [64], replicated, may hold values from 0.5 to 2
- slot_band: int32 [128], replicated, may hold values from -1 to 63, as said below
Outputs:
- band_signals: float32 [128, 16384], P(('tx', 'ty'))
The draws below stay inside these ranges and needn't reach their ends.
Inputs may be any that keep to these rules, and one draw needn't show every extreme that they name: `band_width`: every band's width lies between 2048 and 16384; some band has exactly 16384 bins. `slot_band`: slots d * 4 to d * 4 + 3 belong to device d; every band stands in exactly one slot, the others hold -1; in every draw some device has all its 4 slots filled.
All inputs are finite; a program needn't handle non-finite values.
Results may differ from the reference program's by a relative error of at most 0.0003.
Values sent between devices are 32-bit elements; how exact they have to be, the bound alone decides.
A program may use at most 64 MiB of HBM per device.

```python
import math
import jax
import jax.numpy as jnp
from jax import lax

BL = 16384
SLOTS = 4
NB = 64
NT = 8388608
N_TX = 4
N_TY = 8


def draw_band_width(key, part):
    first_key, second_key = jax.random.split(key)
    widths = jax.random.randint(first_key, (NB,), BL // 8, BL + 1)
    chosen = jax.random.randint(second_key, (), 0, NB)
    return jnp.where(jnp.arange(NB) == chosen, BL, widths).astype(jnp.int32)


def draw_slot_band(key, part):
    slot_total = N_TX * N_TY * SLOTS
    first_key, second_key = jax.random.split(jax.random.fold_in(key, 7))
    shuffled = jax.random.permutation(first_key, slot_total)
    full_device = jax.random.randint(second_key, (), 0, N_TX * N_TY)
    slot_ids = jnp.arange(slot_total)
    scores = jnp.where(slot_ids // SLOTS == full_device, slot_ids % SLOTS - SLOTS, shuffled)
    ordering = jnp.argsort(scores, stable=True)
    filled = jnp.full((slot_total,), -1, jnp.int32)
    return filled.at[ordering[:NB]].set(jnp.arange(NB, dtype=jnp.int32))


def with_ends(values, stream_key, smallest, top_value):
    index_at = [jax.random.randint(jax.random.fold_in(stream_key, axis), (), 0, length) for axis, length in enumerate(values.shape)]
    main_axis = values.shape.index(max(values.shape))
    next_to = index_at[:main_axis] + [(index_at[main_axis] + 1) % values.shape[main_axis]] + index_at[main_axis + 1:]
    return values.at[tuple(index_at)].set(smallest).at[tuple(next_to)].set(top_value)


def block_scale(key, extent, cuts, low, largest):
    def one(axis_at, shards_of):
        draws = jax.random.uniform(jax.random.fold_in(jax.random.fold_in(key, 6), axis_at), (shards_of,), jnp.float32, low / len(cuts), largest / len(cuts))
        return jnp.repeat(jnp.exp(draws), extent[axis_at] // shards_of).reshape((-1,) + (1,) * (len(extent) - axis_at - 1))

    factor_of = one(*cuts[0])
    for cut in cuts[1:]:
        factor_of = factor_of * one(*cut)
    return factor_of


def scatter_about(own_key, extent, scale, limit, cuts=(), kind=jnp.bfloat16):
    array = scale * jax.random.normal(own_key, extent, jnp.float32)
    if cuts:
        array = array * block_scale(own_key, extent, cuts, -0.22, 0.18)
    return jnp.clip(array, -limit, limit).astype(kind)


def setup_inputs(seed: int = 0) -> dict:
    arg_keys = jax.random.split(jax.random.key(seed), 6)
    signal = scatter_about(arg_keys[0], (NT,), 1.0, 6.0, ((0, 32),), jnp.float32)
    band_start = with_ends(jax.random.randint(arg_keys[1], (NB,), 0, NT - BL - N_TX * N_TY + 1), jax.random.fold_in(arg_keys[1], 1), 0, NT - BL - N_TX * N_TY).astype(jnp.int32)
    band_width = draw_band_width(jax.random.fold_in(arg_keys[5], 71), 0)
    band_gain = jnp.clip(jnp.exp(jax.random.uniform(arg_keys[3], (NB,), jnp.float32, math.log(0.5), math.log(2.0))), 0.5, 2.0)
    slot_band = draw_slot_band(jax.random.fold_in(arg_keys[5], 71), 0)
    return {"signal": signal, "band_start": band_start, "band_width": band_width, "band_gain": band_gain, "slot_band": slot_band}


def reference(signal, band_start, band_width, band_gain, slot_band):
    spectrum = jnp.fft.fft(signal)
    scale_factor = 1.0 / math.sqrt(NT)
    hartley = (spectrum.real - spectrum.imag).astype(signal.dtype) * scale_factor
    two_pi = 2.0 * math.pi

    def one_band(start, width, gain):
        segment = lax.dynamic_slice(hartley, (start,), (BL,))
        bin_index = jnp.arange(BL).astype(hartley.dtype)
        width_value = width.astype(hartley.dtype)
        taper_gain = jnp.where(bin_index < width_value, 0.5 - 0.5 * jnp.cos(two_pi * (bin_index + 0.5) / width_value), 0.0)
        band_spectrum = jnp.fft.fft(segment * taper_gain)
        return (band_spectrum.real - band_spectrum.imag).astype(hartley.dtype) * (gain / jnp.sqrt(width_value))
    all_bands = jax.vmap(one_band)(band_start, band_width, band_gain)
    safe_index = jnp.maximum(slot_band, 0)
    picked = all_bands[safe_index]
    return jnp.where((slot_band >= 0)[:, None], picked, 0.0).astype(jnp.float32)
```

```python
import math

import jax
import jax.numpy as jnp
import numpy as np
from jax import lax
from jax.sharding import PartitionSpec as P

BL = 16384
RAD = 256
VL = BL // RAD

two_pi = 2.0 * math.pi
AXES = ("tx", "ty")


def grid(first, second, modulus):
    return (two_pi / modulus) * (np.outer(first, second) % modulus)


def const(array):
    return jnp.asarray(np.ascontiguousarray(array, dtype=np.float32))


def dot(spec, left, right):
    return jnp.einsum(spec, left, right, precision=lax.Precision.HIGH)


def exchange(blocks):
    return lax.all_to_all(blocks, AXES, split_axis=0, concat_axis=0, tiled=True)


def lookup(values_table, positions):
    one_hot = positions[:, None] == jnp.arange(values_table.shape[0], dtype=jnp.int32)[None, :]
    return jnp.sum(
        jnp.where(one_hot, values_table[None, :], jnp.zeros((), values_table.dtype)), axis=1
    )


def row_bases(devices):
    half = RAD // (2 * devices)
    base = np.zeros((devices, 2, half), np.int64)
    for f in range(devices):
        for i in range(half):
            base[f, :, i] = f + 2 * devices * i if f else devices * i
    base[0, 1, 0] = RAD // 2
    return base


def body(signal, band_start, band_width, band_gain, slot_band):
    devices = lax.axis_size("tx") * lax.axis_size("ty")
    device = lax.axis_index("tx") * lax.axis_size("ty") + lax.axis_index("ty")
    length = signal.shape[0]
    total = length * devices
    own = length // (RAD * RAD)
    cols = own * devices
    chunk = length // cols
    base = row_bases(devices)
    half = base.shape[2]
    span = np.arange(RAD)

    turned = signal.reshape(chunk, cols).T.reshape(devices, own, chunk)
    column = exchange(turned)
    column = column.reshape(devices, own, chunk // RAD, RAD).transpose(1, 0, 2, 3).reshape(own, RAD, RAD)

    angle = grid(base.reshape(-1), span, RAD)
    section_real = dot("rp,cpz->crz", const(np.cos(angle)), column)
    section_imag = dot("rp,cpz->crz", const(-np.sin(angle)), column)
    angle = grid(base.reshape(-1), span, RAD * RAD)
    twist_cos, twist_sin = const(np.cos(angle)), const(np.sin(angle))
    turned_real = section_real * twist_cos + section_imag * twist_sin
    turned_imag = section_imag * twist_cos - section_real * twist_sin
    both = jnp.concatenate([turned_real, turned_imag], axis=2).reshape(own, devices, 2, half, 2 * RAD)
    angle = grid(span, span, RAD)
    cos_m, sin_m = np.cos(angle), np.sin(angle)
    minus = np.concatenate([cos_m + sin_m, sin_m - cos_m], axis=0)
    plus = np.concatenate([cos_m - sin_m, cos_m + sin_m], axis=0)
    bins = dot("cfhiz,hzq->fchiq", both, const(np.stack([minus, plus]) / math.sqrt(total)))

    value = exchange(bins).reshape(cols, 2, half, RAD)

    is_first = device == 0
    swap0 = np.zeros((RAD, RAD))
    swap0[(-span) % RAD, span] = 1.0
    swap1 = np.zeros((RAD, RAD))
    swap1[RAD - 1 - span, span] = 1.0
    own0 = jnp.einsum("cq,qr->cr", value[:, 0, 0], const(swap0), precision=lax.Precision.HIGHEST)
    own1 = jnp.einsum("cq,qr->cr", value[:, 1, 0], const(swap1), precision=lax.Precision.HIGHEST)
    other = value[:, ::-1]
    other = other.at[:, 0, 0].set(jnp.where(is_first, own0, other[:, 0, 0]))
    other = other.at[:, 1, 0].set(jnp.where(is_first, own1, other[:, 1, 0]))
    my_base = lax.dynamic_index_in_dim(jnp.asarray(base.astype(np.int32)), device, 0, keepdims=False)
    col = np.arange(cols)
    beta = (jnp.asarray(col.astype(np.int32))[:, None, None] * my_base[None]).astype(jnp.float32) * (two_pi / total)
    beta_cos, beta_sin = jnp.cos(beta)[..., None], jnp.sin(beta)[..., None]
    alpha = grid(col, RAD * span, total)
    alpha_cos, alpha_sin = const(np.cos(alpha))[:, None, None], const(np.sin(alpha))[:, None, None]
    theta_cos = alpha_cos * beta_cos - alpha_sin * beta_sin
    theta_sin = alpha_sin * beta_cos + alpha_cos * beta_sin
    sign = const(np.array([1.0, -1.0]))[None, :, None, None]
    signed = sign * other
    lead = theta_cos * value + theta_sin * signed
    trail = theta_cos * signed - theta_sin * value
    angle = grid(col, col, cols)
    table = dot("gc,chiq->hgqi", const(np.cos(angle)), lead) + dot(
        "gc,chiq->hgqi", const(np.sin(angle)), trail
    )

    rows = total // RAD
    slot_index = jnp.maximum(slot_band, 0)
    starts = lookup(band_start, slot_index)
    first = starts // RAD
    remain = starts % RAD
    table = table.reshape(2, rows, half)
    begin = jnp.stack([first, rows - 1 - first - VL])
    take = lambda part, at: lax.dynamic_slice(part, (at, 0), (VL + 1, half))
    window = jax.vmap(lambda part, at: jax.vmap(lambda a: take(part, a))(at))(table, begin)
    residue = (my_base * jnp.asarray([[1], [-1]], jnp.int32)) % RAD
    wraps = residue[:, None, :] < remain[None, :, None]
    ahead = jnp.concatenate([jnp.where(wraps[0], window[0, :, VL], window[0, :, 0])[:, None], window[0, :, 1:VL]], axis=1)
    back = jnp.concatenate([window[1, :, 1:VL], jnp.where(wraps[1], window[1, :, 0], window[1, :, VL])[:, None]], axis=1)
    slots = slot_band.shape[0] // devices
    outgoing = jnp.stack([ahead, back], axis=1).transpose(0, 1, 3, 2).reshape(devices, slots, 2, half, VL)
    incoming = exchange(outgoing)

    mine = lambda array: lax.dynamic_slice_in_dim(array, device * slots, slots)
    my_slots = mine(slot_band)
    my_index = jnp.maximum(my_slots, 0)
    my_start, my_remain = mine(starts), mine(remain)
    my_width = lookup(band_width, my_index).astype(jnp.float32)
    my_gain = lookup(band_gain, my_index)
    all_residue = (base * np.array([1, -1])[None, :, None]) % RAD
    step = np.stack([np.arange(VL), VL - 1 - np.arange(VL)])
    place = step[None, :, None, :] * RAD + all_residue[..., None]
    position = (jnp.asarray(place.astype(np.int32))[:, None] - my_remain[None, :, None, None, None]) % BL
    position = position.astype(jnp.float32)
    wide = my_width[None, :, None, None, None]
    taper_gain = jnp.where(
        position < wide, 0.5 - 0.5 * jnp.cos(two_pi * (position + 0.5) / wide), 0.0
    )
    tapered = incoming * taper_gain
    angle = np.stack([grid(step[0], np.arange(VL), VL), grid(step[1], np.arange(VL), VL)])
    part_real = dot("fshiv,hvt->sfhit", tapered, const(np.cos(angle)))
    part_imag = dot("fshiv,hvt->sfhit", tapered, const(-np.sin(angle)))
    angle = grid(all_residue.reshape(-1), np.arange(VL), BL).reshape(base.shape + (VL,))
    twist_cos, twist_sin = const(np.cos(angle)), const(np.sin(angle))
    turned_real = (part_real * twist_cos + part_imag * twist_sin).reshape(slots, RAD, VL)
    turned_imag = (part_imag * twist_cos - part_real * twist_sin).reshape(slots, RAD, VL)
    stacked = jnp.concatenate([turned_real, turned_imag], axis=1)
    angle = grid(span, all_residue.reshape(-1), RAD)
    cos_m, sin_m = np.cos(angle), np.sin(angle)
    real = dot("ur,srt->sut", const(np.concatenate([cos_m, sin_m], axis=1)), stacked)
    imag = dot("ur,srt->sut", const(np.concatenate([-sin_m, cos_m], axis=1)), stacked)
    when = jnp.arange(BL, dtype=jnp.int32).reshape(RAD, VL)
    phase = (my_remain[:, None, None] * when[None] % BL).astype(jnp.float32) * (two_pi / BL)
    phase_cos, phase_sin = jnp.cos(phase), jnp.sin(phase)
    result = real * (phase_cos - phase_sin) - imag * (phase_sin + phase_cos)
    scale = jnp.where(my_slots >= 0, my_gain / jnp.sqrt(my_width), 0.0)
    return (result * scale[:, None, None]).reshape(slots, BL)


def solution(mesh):
    return jax.shard_map(
        body,
        mesh=mesh,
        in_specs=(P(AXES), P(), P(), P(), P()),
        out_specs=P(AXES, None),
        check_vma=False,
    )
```

```python
import math

import jax
import jax.numpy as jnp
import numpy as np
from jax import lax
from jax.experimental import pallas as pl
from jax.experimental.pallas import tpu as pltpu
from jax.sharding import PartitionSpec as P

BL = 16384
RAD = 256
VL = BL // RAD

two_pi = 2.0 * math.pi
AXES = ("tx", "ty")


def grid(first, second, modulus):
    return (two_pi / modulus) * (np.outer(first, second) % modulus)


def const(array):
    return jnp.asarray(np.ascontiguousarray(array, dtype=np.float32))


def dot(spec, left, right):
    return jnp.einsum(spec, left, right, precision=lax.Precision.HIGH)


def exchange(blocks):
    return lax.all_to_all(blocks, AXES, split_axis=0, concat_axis=0, tiled=True)


def lookup(values_table, positions):
    one_hot = positions[:, None] == jnp.arange(values_table.shape[0], dtype=jnp.int32)[None, :]
    return jnp.sum(
        jnp.where(one_hot, values_table[None, :], jnp.zeros((), values_table.dtype)), axis=1
    )


def row_bases(devices):
    half = RAD // (2 * devices)
    base = np.zeros((devices, 2, half), np.int64)
    for f in range(devices):
        for i in range(half):
            base[f, :, i] = f + 2 * devices * i if f else devices * i
    base[0, 1, 0] = RAD // 2
    return base


def split(array):
    high = array.astype(jnp.bfloat16)
    return high, (array - high.astype(jnp.float32)).astype(jnp.bfloat16)


def const_split(array):
    array = np.ascontiguousarray(array, dtype=np.float32)
    high = array.astype(jnp.bfloat16)
    return jnp.asarray(np.stack([high, (array - high.astype(np.float32)).astype(jnp.bfloat16)]))


def product(left, right):
    (left_high, left_low), (right_high, right_low) = left, right
    one = lambda a, b: jnp.dot(a, b, preferred_element_type=jnp.float32)
    return one(left_high, right_high) + (one(left_high, right_low) + one(left_low, right_high))


def combine_kernel(
    own, half, total, device_ref, start_ref, value_ref, alpha_ref, beta_ref, mix_ref, swap_ref, residue_ref,
    out_ref, table_ref,
):
    rows = total // RAD
    count = value_ref.shape[0]
    cols = count // 2
    tiles = rows // (2 * VL)
    is_upper = lax.broadcasted_iota(jnp.int32, (count, RAD), 0) // own % 2 == 1

    def exchange_rows(block):
        cut = block.reshape(count // (2 * own), 2, own, RAD)
        return jnp.concatenate([cut[:, 1:], cut[:, :1]], axis=1).reshape(count, RAD)

    def twist(block, at):
        beta_cos, beta_sin = beta_ref[0, :, at : at + 1], beta_ref[1, :, at : at + 1]
        theta_cos = alpha_ref[0] * beta_cos - alpha_ref[1] * beta_sin
        theta_sin = alpha_ref[1] * beta_cos + alpha_ref[0] * beta_sin
        return theta_cos * block + theta_sin * exchange_rows(block)

    mix = mix_ref[0], mix_ref[1]

    def put(result, h, i):
        for side in range(2):
            at = pl.ds(8 * side + h * half + i, cols, stride=16)
            table_ref[at, :] = result[:, side * 128 : (side + 1) * 128]

    for i in range(half):
        result = product(mix, split(twist(value_ref[:, i * RAD : (i + 1) * RAD], i)))
        for h in range(2):
            put(result[h * cols : (h + 1) * cols], h, i)

    @pl.when(device_ref[0] == 0)
    def _():
        block = value_ref[:, :RAD]
        high, low = split(block)
        for h in range(2):
            turn = lambda part: jnp.dot(part, swap_ref[h], preferred_element_type=jnp.float32)
            mirror = exchange_rows(turn(high) + turn(low))
            keep = is_upper if h else ~is_upper
            spun = split(twist(jnp.where(keep, block, mirror), h * half))
            rows_of = slice(h * cols, (h + 1) * cols)
            put(product((mix_ref[0, rows_of], mix_ref[1, rows_of]), spun), h, 0)

    shape = (2 * half, 128)
    lane = lax.broadcasted_iota(jnp.int32, shape, 1)
    is_low = lane < VL
    is_back = lax.broadcasted_iota(jnp.int32, shape, 0) >= half
    residue = residue_ref[...]

    def load(tile):
        return table_ref[pl.ds(pl.multiple_of(tile * 8, 8), 8), :][: 2 * half]

    def window(slot):
        start = start_ref[slot]
        block = start // BL
        back = rows // VL - 2 - block
        tiles_of = [block // 2, (block + 1) // 2, back // 2, (back + 1) // 2]
        ahead_high, ahead_low, back_high, back_low = [load(t) for t in tiles_of]
        picked = jnp.where(is_low, jnp.where(is_back, back_low, ahead_low), jnp.where(is_back, back_high, ahead_high))
        ahead_at = 128 * jnp.where(is_low, tiles_of[1], tiles_of[0]) + lane
        back_at = rows - 1 - (128 * jnp.where(is_low, tiles_of[3], tiles_of[2]) + lane)
        place = RAD * jnp.where(is_back, back_at, ahead_at) + residue - start
        picked = jnp.where((place >= 0) & (place < BL), picked, 0.0)
        return picked + pltpu.roll(picked, VL, 1)

    def step(pair, carry):
        out_ref[pair] = jnp.where(is_low, window(2 * pair), window(2 * pair + 1))
        return carry

    lax.fori_loop(0, out_ref.shape[0], step, 0, unroll=4)


def combine(value, starts, device, base, own, total):
    devices, _, half = base.shape
    count = value.shape[0]
    cols = count // 2
    span = np.arange(RAD)
    col = np.arange(cols)
    sign = np.array([1.0, -1.0])[None, :, None]

    def rows_of(angle):
        part = angle.reshape(devices, 1, own, -1)
        put = lambda array: np.broadcast_to(array, (devices, 2, own, part.shape[-1])).reshape(count, -1)
        return np.stack([put(np.cos(part)), put(sign[..., None] * np.sin(part))]).astype(np.float32)

    alpha = rows_of(grid(col, RAD * span, total))
    at = np.concatenate([base[:, 0], base[:, 1, :1]], axis=1).astype(np.int32)
    at = lax.dynamic_index_in_dim(jnp.asarray(at), device, 0, keepdims=False)
    col_of = np.broadcast_to(col.reshape(devices, 1, own), (devices, 2, own)).reshape(count, 1)
    sign_of = np.broadcast_to(np.array([1.0, -1.0])[:, None], (devices, 2, own)).reshape(count, 1)
    angle = (jnp.asarray(col_of.astype(np.int32)) * at[None]).astype(jnp.float32) * (two_pi / total)
    beta = jnp.stack([jnp.cos(angle), const(sign_of) * jnp.sin(angle)])
    angle = grid(col, col, cols).reshape(cols, devices, 1, own)
    ahead = np.concatenate([np.cos(angle), np.sin(angle)], axis=2)
    back = np.concatenate([-np.sin(angle), np.cos(angle)], axis=2)
    mix = np.stack([ahead, back]).reshape(count, count)
    swap = np.zeros((2, RAD, RAD))
    swap[0, (-span) % RAD, span] = 1.0
    swap[1, RAD - 1 - span, span] = 1.0
    residue = ((base * np.array([1, -1])[None, :, None]) % RAD).reshape(devices, 2 * half, 1)
    residue = jnp.asarray(np.broadcast_to(residue, (devices, 2 * half, 128)).astype(np.int32))
    residue = lax.dynamic_index_in_dim(residue, device, 0, keepdims=False)
    smem = pl.BlockSpec(memory_space=pltpu.SMEM)
    vmem = pl.BlockSpec(memory_space=pltpu.VMEM)
    rows = total // RAD
    return pl.pallas_call(
        lambda *refs: combine_kernel(own, half, total, *refs),
        out_shape=jax.ShapeDtypeStruct((starts.shape[0] // 2, 2 * half, 128), jnp.float32),
        in_specs=[smem, smem] + [vmem] * 6,
        out_specs=vmem,
        scratch_shapes=[pltpu.VMEM((rows // 16, 128), jnp.float32)],
        compiler_params=pltpu.CompilerParams(vmem_limit_bytes=48 * 1024 * 1024),
        name="combine",
    )(
        device.reshape(1).astype(jnp.int32), starts, value, const(alpha), beta, const_split(mix),
        jnp.asarray(swap.astype(np.float32).astype(jnp.bfloat16)), residue,
    )


def body(signal, band_start, band_width, band_gain, slot_band):
    devices = lax.axis_size("tx") * lax.axis_size("ty")
    device = lax.axis_index("tx") * lax.axis_size("ty") + lax.axis_index("ty")
    length = signal.shape[0]
    total = length * devices
    own = length // (RAD * RAD)
    cols = own * devices
    chunk = length // cols
    base = row_bases(devices)
    half = base.shape[2]
    span = np.arange(RAD)

    turned = signal.reshape(chunk, cols).T.reshape(devices, own, chunk)
    column = exchange(turned)
    column = column.reshape(devices, own, chunk // RAD, RAD).transpose(1, 0, 2, 3).reshape(own, RAD, RAD)

    angle = grid(base.reshape(-1), span, RAD)
    section_real = dot("rp,cpz->crz", const(np.cos(angle)), column)
    section_imag = dot("rp,cpz->crz", const(-np.sin(angle)), column)
    angle = grid(base.reshape(-1), span, RAD * RAD)
    twist_cos, twist_sin = const(np.cos(angle)), const(np.sin(angle))
    turned_real = section_real * twist_cos + section_imag * twist_sin
    turned_imag = section_imag * twist_cos - section_real * twist_sin
    both = jnp.concatenate([turned_real, turned_imag], axis=2).reshape(own, devices, 2, half, 2 * RAD)
    angle = grid(span, span, RAD)
    cos_m, sin_m = np.cos(angle), np.sin(angle)
    minus = np.concatenate([cos_m + sin_m, sin_m - cos_m], axis=0)
    plus = np.concatenate([cos_m - sin_m, cos_m + sin_m], axis=0)
    bins = dot("cfhiz,hzq->fhciq", both, const(np.stack([minus, plus]) / math.sqrt(total)))

    value = exchange(bins).reshape(2 * cols, half * RAD)

    slot_index = jnp.maximum(slot_band, 0)
    starts = lookup(band_start, slot_index)
    outgoing = combine(value, starts, device, base, own, total)
    slots = slot_band.shape[0] // devices
    incoming = exchange(outgoing.reshape(devices, slots // 2, 2 * half, 2 * VL))
    incoming = incoming.reshape(devices, slots // 2, 2, half, 2, VL)

    mine = lambda array: lax.dynamic_slice_in_dim(array, device * slots, slots)
    my_slots = mine(slot_band)
    my_index = jnp.maximum(my_slots, 0)
    my_remain = mine(starts) % BL
    my_width = lookup(band_width, my_index).astype(jnp.float32)
    my_gain = lookup(band_gain, my_index)
    all_residue = (base * np.array([1, -1])[None, :, None]) % RAD
    step = np.stack([np.arange(VL), VL - 1 - np.arange(VL)])
    place = step[None, :, None, :] * RAD + all_residue[..., None]
    place = jnp.asarray(place.astype(np.int32))[:, None, :, :, None]
    pairs = lambda array: array.reshape(1, slots // 2, 1, 1, 2, 1)
    position = ((place - pairs(my_remain)) % BL).astype(jnp.float32)
    wide = pairs(my_width)
    taper_gain = jnp.where(
        position < wide, 0.5 - 0.5 * jnp.cos(two_pi * (position + 0.5) / wide), 0.0
    )
    tapered = incoming * taper_gain
    angle = np.stack([grid(step[0], np.arange(VL), VL), grid(step[1], np.arange(VL), VL)])
    part_real = dot("fphibv,hvt->pbfhit", tapered, const(np.cos(angle)))
    part_imag = dot("fphibv,hvt->pbfhit", tapered, const(-np.sin(angle)))
    angle = grid(all_residue.reshape(-1), np.arange(VL), BL).reshape(base.shape + (VL,))
    twist_cos, twist_sin = const(np.cos(angle)), const(np.sin(angle))
    turned_real = (part_real * twist_cos + part_imag * twist_sin).reshape(slots, RAD, VL)
    turned_imag = (part_imag * twist_cos - part_real * twist_sin).reshape(slots, RAD, VL)
    stacked = jnp.concatenate([turned_real, turned_imag], axis=1)
    angle = grid(span, all_residue.reshape(-1), RAD)
    cos_m, sin_m = np.cos(angle), np.sin(angle)
    real = dot("ur,srt->sut", const(np.concatenate([cos_m, sin_m], axis=1)), stacked)
    imag = dot("ur,srt->sut", const(np.concatenate([-sin_m, cos_m], axis=1)), stacked)
    when = jnp.arange(BL, dtype=jnp.int32).reshape(RAD, VL)
    phase = (my_remain[:, None, None] * when[None] % BL).astype(jnp.float32) * (two_pi / BL)
    phase_cos, phase_sin = jnp.cos(phase), jnp.sin(phase)
    result = real * (phase_cos - phase_sin) - imag * (phase_sin + phase_cos)
    scale = jnp.where(my_slots >= 0, my_gain / jnp.sqrt(my_width), 0.0)
    return (result * scale[:, None, None]).reshape(slots, BL)


def solution(mesh):
    return jax.shard_map(
        body,
        mesh=mesh,
        in_specs=(P(AXES), P(), P(), P(), P()),
        out_specs=P(AXES, None),
        check_vma=False,
    )
```

```python
import math

import jax
import jax.numpy as jnp
import numpy as np
from jax import lax
from jax.experimental import pallas as pl
from jax.experimental.pallas import tpu as pltpu
from jax.sharding import PartitionSpec as P

BL = 16384
RAD = 256
VL = BL // RAD

two_pi = 2.0 * math.pi
AXES = ("tx", "ty")


def grid(first, second, modulus):
    return (two_pi / modulus) * (np.outer(first, second) % modulus)


def const(array):
    return jnp.asarray(np.ascontiguousarray(array, dtype=np.float32))


def dot(spec, left, right):
    return jnp.einsum(spec, left, right, precision=lax.Precision.HIGH)


def lookup(values_table, positions):
    one_hot = positions[:, None] == jnp.arange(values_table.shape[0], dtype=jnp.int32)[None, :]
    return jnp.sum(
        jnp.where(one_hot, values_table[None, :], jnp.zeros((), values_table.dtype)), axis=1
    )


def row_bases(devices):
    half = RAD // (2 * devices)
    base = np.zeros((devices, 2, half), np.int64)
    for f in range(devices):
        for i in range(half):
            base[f, :, i] = f + 2 * devices * i if f else devices * i
    base[0, 1, 0] = RAD // 2
    return base


def split(array):
    high = array.astype(jnp.bfloat16)
    return high, (array - high.astype(jnp.float32)).astype(jnp.bfloat16)


def const_split(array):
    array = np.ascontiguousarray(array, dtype=np.float32)
    high = array.astype(jnp.bfloat16)
    return jnp.asarray(np.stack([high, (array - high.astype(np.float32)).astype(jnp.bfloat16)]))


def product(left, right):
    (left_high, left_low), (right_high, right_low) = left, right
    one = lambda a, b: jnp.dot(a, b, preferred_element_type=jnp.float32)
    return one(left_high, right_high) + (one(left_high, right_low) + one(left_low, right_high))


def meet(size_x, size_y, send_sem, recv_sem):
    devices = size_x * size_y
    me = lax.axis_index("tx") * size_y + lax.axis_index("ty")
    barrier = pltpu.get_barrier_semaphore()

    def greet(j, carry):
        to = lax.rem(me + j, devices)
        pl.semaphore_signal(
            barrier, inc=1, device_id=(to // size_y, lax.rem(to, size_y)), device_id_type=pl.DeviceIdType.MESH
        )
        return carry

    lax.fori_loop(1, devices, greet, 0)
    pl.semaphore_wait(barrier, devices - 1)

    def send(stage, source, target, to):
        pltpu.make_async_remote_copy(
            src_ref=source, dst_ref=target, send_sem=send_sem.at[stage], recv_sem=recv_sem.at[stage],
            device_id=(to // size_y, lax.rem(to, size_y)), device_id_type=pl.DeviceIdType.MESH,
        ).start()

    def wait(ref, sem):
        pltpu.make_async_copy(ref, ref, sem).wait()

    return devices, me, send, wait


def transform_kernel(
    size_x, size_y, own, half,
    turned_ref, first_ref, twist_ref, second_ref,
    value_ref, column_ref, high_ref, low_ref, pass_ref, send_sem, recv_sem,
):
    devices, me, send, wait = meet(size_x, size_y, send_sem, recv_sem)
    others = devices - 1
    high_rows = 2 * own
    span = 2 * half * high_rows

    def send_columns(j, carry):
        to = lax.rem(me + j, devices)
        send(0, turned_ref.at[to], column_ref.at[me], to)
        return carry

    lax.fori_loop(1, devices, send_columns, 0)
    column_ref[me] = turned_ref[me]
    wait(column_ref.at[pl.ds(0, others)], recv_sem.at[0])
    for c in range(own):
        high, low = split(column_ref[:, c].reshape(RAD, RAD))
        high_ref[:, c * RAD : (c + 1) * RAD] = high
        low_ref[:, c * RAD : (c + 1) * RAD] = low

    group = first_ref.shape[0]
    height = half * 8

    def transform(b, carry):
        at = lax.rem(b + me // 8, group)
        section = product((first_ref[at, 0], first_ref[at, 1]), (high_ref[...], low_ref[...]))
        twist_cos, twist_sin = twist_ref[at, 0], twist_ref[at, 1]
        turned = []
        for c in range(own):
            real = section[: 2 * height, c * RAD : (c + 1) * RAD]
            imag = section[2 * height :, c * RAD : (c + 1) * RAD]
            turned.append(
                jnp.concatenate([real * twist_cos + imag * twist_sin, imag * twist_cos - real * twist_sin], axis=1)
            )
        for h in range(2):
            left = jnp.concatenate([part[h * height : (h + 1) * height] for part in turned], axis=0)
            bins = product(split(left), (second_ref[0, h], second_ref[1, h]))
            for c in range(own):
                for i in range(half):
                    row = c * height + i * 8
                    for side in range(2):
                        tile = (2 * i + side) * high_rows
                        pass_ref[pl.ds(at * 8 * span + tile + h * own + c, 8, stride=span), :] = bins[
                            row : row + 8, side * 128 : side * 128 + 128
                        ]
        for j in range(8):
            to = at * 8 + lax.rem(me + j, 8)

            @pl.when(to != me)
            def _():
                part = lambda ref, k: ref.at[pl.ds(pl.multiple_of(k * span, span), span)]
                send(1, part(pass_ref, to), part(value_ref, me), to)

        return carry

    lax.fori_loop(0, group, transform, 0)
    mine = pl.ds(pl.multiple_of(me * span, span), span)
    value_ref[mine, :] = pass_ref[mine, :]
    wait(value_ref.at[pl.ds(0, others * span)], recv_sem.at[1])

    wait(turned_ref.at[pl.ds(0, others)], send_sem.at[0])
    wait(pass_ref.at[pl.ds(0, others * span)], send_sem.at[1])


def combine_kernel(
    devices, own, half, total,
    device_ref, start_ref, value_ref, alpha_ref, beta_ref, mix_ref, swap_ref, residue_ref,
    leave_ref, table_ref,
):
    rows = total // RAD
    count = alpha_ref.shape[1]
    cols = count // 2
    high_rows = 2 * own

    is_upper = lax.broadcasted_iota(jnp.int32, (count, RAD), 0) // own % 2 == 1

    def exchange_rows(block):
        cut = block.reshape(count // (2 * own), 2, own, RAD)
        return jnp.concatenate([cut[:, 1:], cut[:, :1]], axis=1).reshape(count, RAD)

    def twist(block, at):
        beta_cos, beta_sin = beta_ref[0, :, at : at + 1], beta_ref[1, :, at : at + 1]
        theta_cos = alpha_ref[0] * beta_cos - alpha_ref[1] * beta_sin
        theta_sin = alpha_ref[1] * beta_cos + alpha_ref[0] * beta_sin
        return theta_cos * block + theta_sin * exchange_rows(block)

    mix = mix_ref[0], mix_ref[1]

    def values(i):
        part = value_ref[...].reshape(devices, 2 * half, high_rows, 128)
        return jnp.concatenate([part[:, 2 * i + side].reshape(count, 128) for side in range(2)], axis=1)

    def put(result, h, i):
        for side in range(2):
            at = pl.ds(8 * side + h * half + i, cols, stride=16)
            table_ref[at, :] = result[:, side * 128 : (side + 1) * 128]

    for i in range(half):
        result = product(mix, split(twist(values(i), i)))
        for h in range(2):
            put(result[h * cols : (h + 1) * cols], h, i)

    @pl.when(device_ref[0] == 0)
    def _():
        block = values(0)
        high, low = split(block)
        for h in range(2):
            turn = lambda part: jnp.dot(part, swap_ref[h], preferred_element_type=jnp.float32)
            mirror = exchange_rows(turn(high) + turn(low))
            keep = is_upper if h else ~is_upper
            spun = split(twist(jnp.where(keep, block, mirror), h * half))
            rows_of = slice(h * cols, (h + 1) * cols)
            put(product((mix_ref[0, rows_of], mix_ref[1, rows_of]), spun), h, 0)

    shape = (2 * half, 128)
    lane = lax.broadcasted_iota(jnp.int32, shape, 1)
    is_low = lane < VL
    is_back = lax.broadcasted_iota(jnp.int32, shape, 0) >= half
    residue = residue_ref[...]

    def load(tile):
        return table_ref[pl.ds(pl.multiple_of(tile * 8, 8), 8), :][: 2 * half]

    def window(slot):
        start = start_ref[slot]
        block = start // BL
        back = rows // VL - 2 - block
        tiles_of = [block // 2, (block + 1) // 2, back // 2, (back + 1) // 2]
        ahead_high, ahead_low, back_high, back_low = [load(t) for t in tiles_of]
        picked = jnp.where(is_low, jnp.where(is_back, back_low, ahead_low), jnp.where(is_back, back_high, ahead_high))
        ahead_at = 128 * jnp.where(is_low, tiles_of[1], tiles_of[0]) + lane
        back_at = rows - 1 - (128 * jnp.where(is_low, tiles_of[3], tiles_of[2]) + lane)
        place = RAD * jnp.where(is_back, back_at, ahead_at) + residue - start
        picked = jnp.where((place >= 0) & (place < BL), picked, 0.0)
        return picked + pltpu.roll(picked, VL, 1)

    pairs = leave_ref.shape[1]

    def step(to, carry):
        for k in range(pairs):
            slot = 2 * (to * pairs + k)
            leave_ref[to, k] = jnp.where(is_low, window(slot), window(slot + 1))
        return carry

    lax.fori_loop(0, devices, step, 0, unroll=2)


def deliver_kernel(size_x, size_y, leave_ref, out_ref, send_sem, recv_sem):
    devices, me, send, wait = meet(size_x, size_y, send_sem, recv_sem)

    def step(j, carry):
        to = lax.rem(me + j, devices)
        send(0, leave_ref.at[to], out_ref.at[me], to)
        return carry

    lax.fori_loop(1, devices, step, 0)
    out_ref[me] = leave_ref[me]
    wait(leave_ref.at[pl.ds(0, devices - 1)], send_sem.at[0])
    wait(out_ref.at[pl.ds(0, devices - 1)], recv_sem.at[0])


def spectrum(turned, starts, device, base, total):
    size_x, size_y = lax.axis_size("tx"), lax.axis_size("ty")
    devices, _, half = base.shape
    own = turned.shape[1]
    cols = devices * own
    count = 2 * cols
    span = np.arange(RAD)
    col = np.arange(cols)
    sign = np.array([1.0, -1.0])[None, :, None]

    def rows_of(angle):
        part = angle.reshape(devices, 1, own, -1)
        put = lambda array: np.broadcast_to(array, (devices, 2, own, part.shape[-1])).reshape(count, -1)
        return np.stack([put(np.cos(part)), put(sign[..., None] * np.sin(part))]).astype(np.float32)

    alpha = rows_of(grid(col, RAD * span, total))
    at = np.concatenate([base[:, 0], base[:, 1, :1]], axis=1).astype(np.int32)
    at = lax.dynamic_index_in_dim(jnp.asarray(at), device, 0, keepdims=False)
    col_of = np.broadcast_to(col.reshape(devices, 1, own), (devices, 2, own)).reshape(count, 1)
    sign_of = np.broadcast_to(np.array([1.0, -1.0])[:, None], (devices, 2, own)).reshape(count, 1)
    angle = (jnp.asarray(col_of.astype(np.int32)) * at[None]).astype(jnp.float32) * (two_pi / total)
    beta = jnp.stack([jnp.cos(angle), const(sign_of) * jnp.sin(angle)])
    angle = grid(col, col, cols).reshape(cols, devices, 1, own)
    ahead = np.concatenate([np.cos(angle), np.sin(angle)], axis=2)
    back = np.concatenate([-np.sin(angle), np.cos(angle)], axis=2)
    mix = np.stack([ahead, back]).reshape(count, count)
    swap = np.zeros((2, RAD, RAD))
    swap[0, (-span) % RAD, span] = 1.0
    swap[1, RAD - 1 - span, span] = 1.0
    residue = ((base * np.array([1, -1])[None, :, None]) % RAD).reshape(devices, 2 * half, 1)
    residue = jnp.asarray(np.broadcast_to(residue, (devices, 2 * half, 128)).astype(np.int32))
    residue = lax.dynamic_index_in_dim(residue, device, 0, keepdims=False)
    order = base.reshape(devices // 8, 8, 2, half).transpose(0, 2, 3, 1).reshape(devices // 8, -1)
    angle = grid(order.reshape(-1), span, RAD).reshape(order.shape + (RAD,))
    first = np.concatenate([np.cos(angle), -np.sin(angle)], axis=1)
    angle = grid(order.reshape(-1), span, RAD * RAD).reshape(order.shape + (RAD,))
    twist = np.stack([np.cos(angle), np.sin(angle)], axis=1)
    angle = grid(span, span, RAD)
    cos_m, sin_m = np.cos(angle), np.sin(angle)
    minus = np.concatenate([cos_m + sin_m, sin_m - cos_m], axis=0)
    plus = np.concatenate([cos_m - sin_m, cos_m + sin_m], axis=0)
    second = np.stack([minus, plus]) / math.sqrt(total)
    smem = pl.BlockSpec(memory_space=pltpu.SMEM)
    vmem = pl.BlockSpec(memory_space=pltpu.VMEM)
    rows = total // RAD
    pairs = starts.shape[0] // (2 * devices)
    shape = (devices, pairs, 2 * half, 128)
    f32, bf16 = jnp.float32, jnp.bfloat16
    sems = lambda n: [pltpu.SemaphoreType.DMA((n,)), pltpu.SemaphoreType.DMA((n,))]
    limit = 48 * 1024 * 1024
    remote = lambda k: pltpu.CompilerParams(vmem_limit_bytes=limit, collective_id=k, has_side_effects=True)
    value = pl.pallas_call(
        lambda *refs: transform_kernel(size_x, size_y, own, half, *refs),
        out_shape=jax.ShapeDtypeStruct((count * half * 2, 128), f32),
        in_specs=[vmem] * 4,
        out_specs=vmem,
        scratch_shapes=[
            pltpu.VMEM(turned.shape, f32),
            pltpu.VMEM((RAD, own * RAD), bf16),
            pltpu.VMEM((RAD, own * RAD), bf16),
            pltpu.VMEM((count * half * 2, 128), f32),
        ] + sems(2),
        compiler_params=remote(0),
        name="transform",
    )(turned, const_split(first).swapaxes(0, 1), const(twist), const_split(second))
    leaving = pl.pallas_call(
        lambda *refs: combine_kernel(devices, own, half, total, *refs),
        out_shape=jax.ShapeDtypeStruct(shape, f32),
        in_specs=[smem, smem] + [vmem] * 6,
        out_specs=vmem,
        scratch_shapes=[pltpu.VMEM((rows // 16, 128), f32)],
        compiler_params=pltpu.CompilerParams(vmem_limit_bytes=limit),
        name="combine",
    )(
        device.reshape(1).astype(jnp.int32), starts, value, const(alpha), beta,
        const_split(mix), jnp.asarray(swap.astype(np.float32).astype(jnp.bfloat16)), residue,
    )
    return pl.pallas_call(
        lambda *refs: deliver_kernel(size_x, size_y, *refs),
        out_shape=jax.ShapeDtypeStruct(shape, f32),
        in_specs=[vmem],
        out_specs=vmem,
        scratch_shapes=sems(1),
        compiler_params=remote(1),
        name="deliver",
    )(leaving)


def body(signal, band_start, band_width, band_gain, slot_band):
    devices = lax.axis_size("tx") * lax.axis_size("ty")
    device = lax.axis_index("tx") * lax.axis_size("ty") + lax.axis_index("ty")
    length = signal.shape[0]
    total = length * devices
    own = length // (RAD * RAD)
    cols = own * devices
    chunk = length // cols
    base = row_bases(devices)
    half = base.shape[2]

    turned = signal.reshape(chunk // RAD, RAD, cols).transpose(2, 0, 1)
    turned = turned.reshape(devices, own, chunk // RAD, RAD)
    slot_index = jnp.maximum(slot_band, 0)
    starts = lookup(band_start, slot_index)
    incoming = spectrum(turned, starts, device, base, total)
    slots = slot_band.shape[0] // devices

    mine = lambda array: lax.dynamic_slice_in_dim(array, device * slots, slots)
    my_slots = mine(slot_band)
    my_index = jnp.maximum(my_slots, 0)
    my_remain = mine(starts) % BL
    my_width = lookup(band_width, my_index).astype(jnp.float32)
    my_gain = lookup(band_gain, my_index)
    all_residue = (base * np.array([1, -1])[None, :, None]) % RAD
    lane = np.arange(VL)
    step = np.stack([lane, VL - 1 - lane])
    place = step[None, :, None, :] * RAD + all_residue[..., None]
    place = np.tile(place.reshape(devices, 1, 2 * half, VL), (1, 1, 1, 2))
    lanes = lambda array: jnp.repeat(array.reshape(1, slots // 2, 1, 2), VL, axis=3)
    position = ((jnp.asarray(place.astype(np.int32)) - lanes(my_remain)) % BL).astype(jnp.float32)
    wide = lanes(my_width)
    taper_gain = jnp.where(
        position < wide, 0.5 - 0.5 * jnp.cos(two_pi * (position + 0.5) / wide), 0.0
    )
    tapered = (incoming * taper_gain).reshape(devices, slots // 2, 2, half, 2 * VL)
    angle = np.stack([grid(step[0], lane, VL), grid(step[1], lane, VL)])
    twice = lambda array: np.einsum("bd,hvt->hbvdt", np.eye(2), array).reshape(2, 2 * VL, 2 * VL)
    part_real = dot("fphiv,hvt->pfhit", tapered, const(twice(np.cos(angle))))
    part_imag = dot("fphiv,hvt->pfhit", tapered, const(twice(-np.sin(angle))))
    angle = np.tile(grid(all_residue.reshape(-1), lane, BL).reshape(base.shape + (VL,)), (1, 1, 1, 2))
    twist_cos, twist_sin = const(np.cos(angle)), const(np.sin(angle))
    flat = lambda array: array.reshape(slots // 2, RAD, 2 * VL)
    turned_real = flat(part_real * twist_cos + part_imag * twist_sin)
    turned_imag = flat(part_imag * twist_cos - part_real * twist_sin)
    stacked = jnp.concatenate([turned_real, turned_imag], axis=1)
    angle = grid(np.arange(RAD), all_residue.reshape(-1), RAD)
    cos_m, sin_m = np.cos(angle), np.sin(angle)
    real = dot("ur,prt->put", const(np.concatenate([cos_m, sin_m], axis=1)), stacked)
    imag = dot("ur,prt->put", const(np.concatenate([-sin_m, cos_m], axis=1)), stacked)
    when = np.tile(np.arange(BL).reshape(1, RAD, VL), (1, 1, 2))
    lanes = lambda array: jnp.repeat(array.reshape(slots // 2, 1, 2), VL, axis=2)
    phase = (lanes(my_remain) * jnp.asarray(when.astype(np.int32)) % BL).astype(jnp.float32) * (two_pi / BL)
    phase_cos, phase_sin = jnp.cos(phase), jnp.sin(phase)
    scale = jnp.where(my_slots >= 0, my_gain / jnp.sqrt(my_width), 0.0)
    result = (real * (phase_cos - phase_sin) - imag * (phase_sin + phase_cos)) * lanes(scale)
    result = result.reshape(slots // 2, RAD, 2, VL).transpose(0, 2, 1, 3)
    return result.reshape(slots, BL)


def solution(mesh):
    return jax.shard_map(
        body,
        mesh=mesh,
        in_specs=(P(AXES), P(), P(), P(), P()),
        out_specs=P(AXES, None),
        check_vma=False,
    )
```

```python
import math

import jax
import jax.numpy as jnp
import numpy as np
from jax import lax
from jax.experimental import pallas as pl
from jax.experimental.pallas import tpu as pltpu
from jax.sharding import PartitionSpec as P

BL = 16384
RAD = 256
VL = BL // RAD

two_pi = 2.0 * math.pi
AXES = ("tx", "ty")


def grid(first, second, modulus):
    return (two_pi / modulus) * (np.outer(first, second) % modulus)


def const(array):
    return jnp.asarray(np.ascontiguousarray(array, dtype=np.float32))


def lookup(values_table, positions):
    one_hot = positions[:, None] == jnp.arange(values_table.shape[0], dtype=jnp.int32)[None, :]
    return jnp.sum(
        jnp.where(one_hot, values_table[None, :], jnp.zeros((), values_table.dtype)), axis=1
    )


def row_bases(devices):
    half = RAD // (2 * devices)
    base = np.zeros((devices, 2, half), np.int64)
    for f in range(devices):
        for i in range(half):
            base[f, :, i] = f + 2 * devices * i if f else devices * i
    base[0, 1, 0] = RAD // 2
    return base


def split(array):
    high = array.astype(jnp.bfloat16)
    return high, (array - high.astype(jnp.float32)).astype(jnp.bfloat16)


def const_split(array):
    array = np.ascontiguousarray(array, dtype=np.float32)
    high = array.astype(jnp.bfloat16)
    return jnp.asarray(np.stack([high, (array - high.astype(np.float32)).astype(jnp.bfloat16)]))


def product(left, right):
    (left_high, left_low), (right_high, right_low) = left, right
    one = lambda a, b: jnp.dot(a, b, preferred_element_type=jnp.float32)
    return one(left_high, right_high) + (one(left_high, right_low) + one(left_low, right_high))


def meet(size_x, size_y, send_sem, recv_sem):
    devices = size_x * size_y
    me = lax.axis_index("tx") * size_y + lax.axis_index("ty")
    barrier = pltpu.get_barrier_semaphore()

    def greet(j, carry):
        to = lax.rem(me + j, devices)
        pl.semaphore_signal(
            barrier, inc=1, device_id=(to // size_y, lax.rem(to, size_y)), device_id_type=pl.DeviceIdType.MESH
        )
        return carry

    lax.fori_loop(1, devices, greet, 0)
    pl.semaphore_wait(barrier, devices - 1)

    def send(stage, source, target, to):
        pltpu.make_async_remote_copy(
            src_ref=source, dst_ref=target, send_sem=send_sem.at[stage], recv_sem=recv_sem.at[stage],
            device_id=(to // size_y, lax.rem(to, size_y)), device_id_type=pl.DeviceIdType.MESH,
        ).start()

    def wait(ref, sem):
        pltpu.make_async_copy(ref, ref, sem).wait()

    return devices, me, send, wait


def fetch(sem, *pairs):
    loads = [pltpu.make_async_copy(source, target, sem.at[k]) for k, (source, target) in enumerate(pairs)]
    for load in loads:
        load.start()
    return loads


def transform_kernel(
    size_x, size_y, own, half,
    turned_ref, first_hbm, twist_hbm, second_hbm,
    value_ref, column_ref, high_ref, low_ref, pass_ref, first_ref, twist_ref, second_ref,
    send_sem, recv_sem, load_sem,
):
    devices, me, send, wait = meet(size_x, size_y, send_sem, recv_sem)
    others = devices - 1
    high_rows = 2 * own
    span = 2 * half * high_rows

    def send_columns(j, carry):
        to = lax.rem(me + j, devices)
        send(0, turned_ref.at[to], column_ref.at[me], to)
        return carry

    lax.fori_loop(1, devices, send_columns, 0)
    loads = fetch(
        load_sem, (turned_ref.at[me], column_ref.at[me]),
        (first_hbm, first_ref), (twist_hbm, twist_ref), (second_hbm, second_ref),
    )
    for load in loads:
        load.wait()
    wait(column_ref.at[pl.ds(0, others)], recv_sem.at[0])
    for c in range(own):
        high, low = split(column_ref[:, c].reshape(RAD, RAD))
        high_ref[:, c * RAD : (c + 1) * RAD] = high
        low_ref[:, c * RAD : (c + 1) * RAD] = low

    group = first_ref.shape[0]
    height = half * 8

    def transform(b, carry):
        at = lax.rem(b + me // 8, group)
        section = product((first_ref[at, 0], first_ref[at, 1]), (high_ref[...], low_ref[...]))
        twist_cos, twist_sin = twist_ref[at, 0], twist_ref[at, 1]
        turned = []
        for c in range(own):
            real = section[: 2 * height, c * RAD : (c + 1) * RAD]
            imag = section[2 * height :, c * RAD : (c + 1) * RAD]
            turned.append(
                jnp.concatenate([real * twist_cos + imag * twist_sin, imag * twist_cos - real * twist_sin], axis=1)
            )
        for h in range(2):
            left = jnp.concatenate([part[h * height : (h + 1) * height] for part in turned], axis=0)
            bins = product(split(left), (second_ref[0, h], second_ref[1, h]))
            for c in range(own):
                for i in range(half):
                    row = c * height + i * 8
                    for side in range(2):
                        tile = (2 * i + side) * high_rows
                        pass_ref[pl.ds(at * 8 * span + tile + h * own + c, 8, stride=span), :] = bins[
                            row : row + 8, side * 128 : side * 128 + 128
                        ]
        for j in range(8):
            to = at * 8 + lax.rem(me + j, 8)

            @pl.when(to != me)
            def _():
                part = lambda ref, k: ref.at[pl.ds(pl.multiple_of(k * span, span), span)]
                send(1, part(pass_ref, to), part(value_ref, me), to)

        return carry

    lax.fori_loop(0, group, transform, 0)
    mine = pl.ds(pl.multiple_of(me * span, span), span)
    value_ref[mine, :] = pass_ref[mine, :]
    wait(value_ref.at[pl.ds(0, others * span)], recv_sem.at[1])

    wait(turned_ref.at[pl.ds(0, others)], send_sem.at[0])
    wait(pass_ref.at[pl.ds(0, others * span)], send_sem.at[1])


def combine_kernel(
    devices, own, half, total,
    device_ref, start_ref, value_ref, alpha_ref, beta_ref, mix_ref, swap_ref, residue_ref,
    leave_ref, table_ref,
):
    rows = total // RAD
    count = alpha_ref.shape[1]
    cols = count // 2
    high_rows = 2 * own

    is_upper = lax.broadcasted_iota(jnp.int32, (count, RAD), 0) // own % 2 == 1

    def exchange_rows(block):
        cut = block.reshape(count // (2 * own), 2, own, RAD)
        return jnp.concatenate([cut[:, 1:], cut[:, :1]], axis=1).reshape(count, RAD)

    def twist(block, at):
        beta_cos, beta_sin = beta_ref[0, :, at : at + 1], beta_ref[1, :, at : at + 1]
        theta_cos = alpha_ref[0] * beta_cos - alpha_ref[1] * beta_sin
        theta_sin = alpha_ref[1] * beta_cos + alpha_ref[0] * beta_sin
        return theta_cos * block + theta_sin * exchange_rows(block)

    mix = mix_ref[0], mix_ref[1]

    def values(i):
        part = value_ref[...].reshape(devices, 2 * half, high_rows, 128)
        return jnp.concatenate([part[:, 2 * i + side].reshape(count, 128) for side in range(2)], axis=1)

    def put(result, h, i):
        for side in range(2):
            at = pl.ds(8 * side + h * half + i, cols, stride=16)
            table_ref[at, :] = result[:, side * 128 : (side + 1) * 128]

    for i in range(half):
        result = product(mix, split(twist(values(i), i)))
        for h in range(2):
            put(result[h * cols : (h + 1) * cols], h, i)

    @pl.when(device_ref[0] == 0)
    def _():
        block = values(0)
        high, low = split(block)
        for h in range(2):
            turn = lambda part: jnp.dot(part, swap_ref[h], preferred_element_type=jnp.float32)
            mirror = exchange_rows(turn(high) + turn(low))
            keep = is_upper if h else ~is_upper
            spun = split(twist(jnp.where(keep, block, mirror), h * half))
            rows_of = slice(h * cols, (h + 1) * cols)
            put(product((mix_ref[0, rows_of], mix_ref[1, rows_of]), spun), h, 0)

    shape = (2 * half, 128)
    lane = lax.broadcasted_iota(jnp.int32, shape, 1)
    is_low = lane < VL
    is_back = lax.broadcasted_iota(jnp.int32, shape, 0) >= half
    residue = residue_ref[...]

    def load(tile):
        return table_ref[pl.ds(pl.multiple_of(tile * 8, 8), 8), :][: 2 * half]

    def window(slot):
        start = start_ref[slot]
        block = start // BL
        back = rows // VL - 2 - block
        tiles_of = [block // 2, (block + 1) // 2, back // 2, (back + 1) // 2]
        ahead_high, ahead_low, back_high, back_low = [load(t) for t in tiles_of]
        picked = jnp.where(is_low, jnp.where(is_back, back_low, ahead_low), jnp.where(is_back, back_high, ahead_high))
        ahead_at = 128 * jnp.where(is_low, tiles_of[1], tiles_of[0]) + lane
        back_at = rows - 1 - (128 * jnp.where(is_low, tiles_of[3], tiles_of[2]) + lane)
        place = RAD * jnp.where(is_back, back_at, ahead_at) + residue - start
        picked = jnp.where((place >= 0) & (place < BL), picked, 0.0)
        return picked + pltpu.roll(picked, VL, 1)

    pairs = leave_ref.shape[1]

    def step(to, carry):
        for k in range(pairs):
            slot = 2 * (to * pairs + k)
            leave_ref[to, k] = jnp.where(is_low, window(slot), window(slot + 1))
        return carry

    lax.fori_loop(0, devices, step, 0, unroll=2)


def deliver_kernel(
    size_x, size_y,
    shift_ref, width_ref, rate_ref, scale_ref, leave_ref, place_hbm, inner_hbm, twist_hbm, outer_hbm, when_hbm,
    out_ref, land_ref, gain_ref, phase_ref, place_ref, inner_ref, twist_ref, outer_ref, when_ref,
    send_sem, recv_sem, load_sem,
):
    devices, me, send, wait = meet(size_x, size_y, send_sem, recv_sem)
    pairs, height = leave_ref.shape[1:3]

    def step(j, carry):
        to = lax.rem(me + j, devices)
        send(0, leave_ref.at[to], land_ref.at[me], to)
        return carry

    lax.fori_loop(1, devices, step, 0)
    loads = fetch(
        load_sem, (place_hbm, place_ref), (when_hbm, when_ref), (inner_hbm, inner_ref), (twist_hbm, twist_ref),
        (outer_hbm, outer_ref),
    )
    land_ref[me] = leave_ref[me]
    for load in loads:
        load.wait()

    is_low = lax.broadcasted_iota(jnp.int32, (1, 128), 1) < VL
    for p in range(pairs):
        of = lambda ref: jnp.where(is_low, ref[2 * p], ref[2 * p + 1])
        shift = of(shift_ref)
        position = (place_ref[...] - shift) & (BL - 1)
        turn = (position.astype(jnp.float32) + 0.5) * of(rate_ref)
        gain_ref[p] = jnp.where(position < of(width_ref), 0.5 - 0.5 * jnp.cos(turn), 0.0)
        angle = ((when_ref[...] * shift) & (BL - 1)).astype(jnp.float32) * (two_pi / BL)
        phase_cos, phase_sin = jnp.cos(angle), jnp.sin(angle)
        phase_ref[p, 0] = (phase_cos - phase_sin) * of(scale_ref)
        phase_ref[p, 1] = (phase_cos + phase_sin) * of(scale_ref)

    wait(land_ref.at[pl.ds(0, devices - 1)], recv_sem.at[0])
    is_back = lax.broadcasted_iota(jnp.int32, (RAD, 1), 0) % height >= height // 2
    stacked = []
    for p in range(pairs):
        tapered = land_ref[:, p].reshape(RAD, 128) * gain_ref[p]
        part = product(split(tapered), (inner_ref[0], inner_ref[1]))
        part = jnp.where(is_back, part[:, 256:], part[:, :256])
        real, imag = part[:, :128], part[:, 128:]
        twist_cos, twist_sin = twist_ref[0], twist_ref[1]
        stacked.append(
            jnp.concatenate([real * twist_cos + imag * twist_sin, imag * twist_cos - real * twist_sin], axis=0)
        )
    result = product((outer_ref[0], outer_ref[1]), split(jnp.concatenate(stacked, axis=1)))
    for p in range(pairs):
        lanes = slice(p * 128, (p + 1) * 128)
        out_ref[p] = result[:RAD, lanes] * phase_ref[p, 0] - result[RAD:, lanes] * phase_ref[p, 1]
    wait(leave_ref.at[pl.ds(0, devices - 1)], send_sem.at[0])


def spectrum(turned, starts, slots, device, base, total):
    size_x, size_y = lax.axis_size("tx"), lax.axis_size("ty")
    devices, _, half = base.shape
    own = turned.shape[1]
    cols = devices * own
    count = 2 * cols
    span = np.arange(RAD)
    col = np.arange(cols)
    sign = np.array([1.0, -1.0])[None, :, None]

    def rows_of(angle):
        part = angle.reshape(devices, 1, own, -1)
        put = lambda array: np.broadcast_to(array, (devices, 2, own, part.shape[-1])).reshape(count, -1)
        return np.stack([put(np.cos(part)), put(sign[..., None] * np.sin(part))]).astype(np.float32)

    alpha = rows_of(grid(col, RAD * span, total))
    at = np.concatenate([base[:, 0], base[:, 1, :1]], axis=1).astype(np.int32)
    at = lax.dynamic_index_in_dim(jnp.asarray(at), device, 0, keepdims=False)
    col_of = np.broadcast_to(col.reshape(devices, 1, own), (devices, 2, own)).reshape(count, 1)
    sign_of = np.broadcast_to(np.array([1.0, -1.0])[:, None], (devices, 2, own)).reshape(count, 1)
    angle = (jnp.asarray(col_of.astype(np.int32)) * at[None]).astype(jnp.float32) * (two_pi / total)
    beta = jnp.stack([jnp.cos(angle), const(sign_of) * jnp.sin(angle)])
    angle = grid(col, col, cols).reshape(cols, devices, 1, own)
    ahead = np.concatenate([np.cos(angle), np.sin(angle)], axis=2)
    back = np.concatenate([-np.sin(angle), np.cos(angle)], axis=2)
    mix = np.stack([ahead, back]).reshape(count, count)
    swap = np.zeros((2, RAD, RAD))
    swap[0, (-span) % RAD, span] = 1.0
    swap[1, RAD - 1 - span, span] = 1.0
    residue = ((base * np.array([1, -1])[None, :, None]) % RAD).reshape(devices, 2 * half, 1)
    residue = jnp.asarray(np.broadcast_to(residue, (devices, 2 * half, 128)).astype(np.int32))
    residue = lax.dynamic_index_in_dim(residue, device, 0, keepdims=False)
    order = base.reshape(devices // 8, 8, 2, half).transpose(0, 2, 3, 1).reshape(devices // 8, -1)
    angle = grid(order.reshape(-1), span, RAD).reshape(order.shape + (RAD,))
    first = np.concatenate([np.cos(angle), -np.sin(angle)], axis=1)
    angle = grid(order.reshape(-1), span, RAD * RAD).reshape(order.shape + (RAD,))
    twist = np.stack([np.cos(angle), np.sin(angle)], axis=1)
    angle = grid(span, span, RAD)
    cos_m, sin_m = np.cos(angle), np.sin(angle)
    minus = np.concatenate([cos_m + sin_m, sin_m - cos_m], axis=0)
    plus = np.concatenate([cos_m - sin_m, cos_m + sin_m], axis=0)
    second = np.stack([minus, plus]) / math.sqrt(total)
    smem = pl.BlockSpec(memory_space=pltpu.SMEM)
    vmem = pl.BlockSpec(memory_space=pltpu.VMEM)
    rows = total // RAD
    pairs = starts.shape[0] // (2 * devices)
    shape = (devices, pairs, 2 * half, 128)
    f32, bf16 = jnp.float32, jnp.bfloat16
    hbm = pl.BlockSpec(memory_space=pl.ANY)
    first, twist, second = const_split(first).swapaxes(0, 1), const(twist), const_split(second)
    room = lambda *arrays: [pltpu.VMEM(array.shape, array.dtype) for array in arrays]
    sems = lambda n: [pltpu.SemaphoreType.DMA((n,)), pltpu.SemaphoreType.DMA((n,))]
    limit = 56 * 1024 * 1024
    remote = lambda k: pltpu.CompilerParams(vmem_limit_bytes=limit, collective_id=k, has_side_effects=True)
    value = pl.pallas_call(
        lambda *refs: transform_kernel(size_x, size_y, own, half, *refs),
        out_shape=jax.ShapeDtypeStruct((count * half * 2, 128), f32),
        in_specs=[hbm] * 4,
        out_specs=vmem,
        scratch_shapes=[
            pltpu.VMEM(turned.shape, f32),
            pltpu.VMEM((RAD, own * RAD), bf16),
            pltpu.VMEM((RAD, own * RAD), bf16),
            pltpu.VMEM((count * half * 2, 128), f32),
        ] + room(first, twist, second) + sems(2) + [pltpu.SemaphoreType.DMA((4,))],
        compiler_params=remote(0),
        name="transform",
    )(turned, first, twist, second)
    leaving = pl.pallas_call(
        lambda *refs: combine_kernel(devices, own, half, total, *refs),
        out_shape=jax.ShapeDtypeStruct(shape, f32),
        in_specs=[smem, smem] + [vmem] * 6,
        out_specs=vmem,
        scratch_shapes=[pltpu.VMEM((rows // 16, 128), f32)],
        compiler_params=pltpu.CompilerParams(vmem_limit_bytes=limit),
        name="combine",
    )(
        device.reshape(1).astype(jnp.int32), starts, value, const(alpha), beta,
        const_split(mix), jnp.asarray(swap.astype(np.float32).astype(jnp.bfloat16)), residue,
    )

    all_residue = (base * np.array([1, -1])[None, :, None]) % RAD
    lane = np.arange(VL)
    back = np.stack([lane, VL - 1 - lane])
    place = back[None, :, None, :] * RAD + all_residue[..., None]
    place = jnp.asarray(np.tile(place.reshape(RAD, VL), (1, 2)).astype(np.int32))
    angle = np.stack([grid(back[0], lane, VL), grid(back[1], lane, VL)])
    both = np.stack([np.cos(angle), -np.sin(angle)])
    inner = const_split(np.einsum("bd,chvt->bvhcdt", np.eye(2), both).reshape(2 * VL, 8 * VL))
    angle = np.tile(grid(all_residue.reshape(-1), lane, BL), (1, 2))
    spin = const(np.stack([np.cos(angle), np.sin(angle)]))
    angle = grid(span, all_residue.reshape(-1), RAD)
    cos_m, sin_m = np.cos(angle), np.sin(angle)
    outer = const_split(np.block([[cos_m, sin_m], [-sin_m, cos_m]]))
    when = jnp.asarray(np.tile(np.arange(BL).reshape(RAD, VL), (1, 2)).astype(np.int32))
    return pl.pallas_call(
        lambda *refs: deliver_kernel(size_x, size_y, *refs),
        out_shape=jax.ShapeDtypeStruct((pairs, RAD, 128), f32),
        in_specs=[smem] * 4 + [vmem] + [hbm] * 5,
        out_specs=vmem,
        scratch_shapes=[
            pltpu.VMEM(shape, f32),
            pltpu.VMEM((pairs, RAD, 128), f32),
            pltpu.VMEM((pairs, 2, RAD, 128), f32),
        ] + room(place, inner, spin, outer, when) + sems(1) + [pltpu.SemaphoreType.DMA((5,))],
        compiler_params=remote(1),
        name="deliver",
    )(*slots, leaving, place, inner, spin, outer, when)


def body(signal, band_start, band_width, band_gain, slot_band):
    devices = lax.axis_size("tx") * lax.axis_size("ty")
    device = lax.axis_index("tx") * lax.axis_size("ty") + lax.axis_index("ty")
    length = signal.shape[0]
    total = length * devices
    own = length // (RAD * RAD)
    cols = own * devices
    chunk = length // cols
    base = row_bases(devices)
    half = base.shape[2]

    turned = signal.reshape(chunk // RAD, RAD, cols).transpose(2, 0, 1)
    turned = turned.reshape(devices, own, chunk // RAD, RAD)
    slot_index = jnp.maximum(slot_band, 0)
    starts = lookup(band_start, slot_index)
    slots = slot_band.shape[0] // devices
    mine = lambda array: lax.dynamic_slice_in_dim(array, device * slots, slots)
    my_slots = mine(slot_band)
    my_index = jnp.maximum(my_slots, 0)
    my_width = lookup(band_width, my_index)
    wide = my_width.astype(jnp.float32)
    scale = jnp.where(my_slots >= 0, lookup(band_gain, my_index) / jnp.sqrt(wide), 0.0)
    result = spectrum(
        turned, starts, (mine(starts) % BL, my_width, two_pi / wide, scale), device, base, total
    )
    result = result.reshape(slots // 2, RAD, 2, VL).transpose(0, 2, 1, 3)
    return result.reshape(slots, BL)


def solution(mesh):
    return jax.shard_map(
        body,
        mesh=mesh,
        in_specs=(P(AXES), P(), P(), P(), P()),
        out_specs=P(AXES, None),
        check_vma=False,
    )
```

```python
import math

import jax
import jax.numpy as jnp
import numpy as np
from jax import lax
from jax.experimental import pallas as pl
from jax.experimental.pallas import tpu as pltpu
from jax.sharding import PartitionSpec as P

BL = 16384
RAD = 256
VL = BL // RAD

two_pi = 2.0 * math.pi
AXES = ("tx", "ty")


def grid(first, second, modulus):
    return (two_pi / modulus) * (np.outer(first, second) % modulus)


def const(array):
    return jnp.asarray(np.ascontiguousarray(array, dtype=np.float32))


def row_bases(devices):
    half = RAD // (2 * devices)
    base = np.zeros((devices, 2, half), np.int64)
    for f in range(devices):
        for i in range(half):
            base[f, :, i] = f + 2 * devices * i if f else devices * i
    base[0, 1, 0] = RAD // 2
    return base


def split(array):
    high = array.astype(jnp.bfloat16)
    return high, (array - high.astype(jnp.float32)).astype(jnp.bfloat16)


def const_split(array):
    array = np.ascontiguousarray(array, dtype=np.float32)
    high = array.astype(jnp.bfloat16)
    return jnp.asarray(np.stack([high, (array - high.astype(np.float32)).astype(jnp.bfloat16)]))


def product(left, right):
    (left_high, left_low), (right_high, right_low) = left, right
    one = lambda a, b: jnp.dot(a, b, preferred_element_type=jnp.float32)
    return one(left_high, right_high) + (one(left_high, right_low) + one(left_low, right_high))


def meet(size_x, size_y, send_sem, recv_sem):
    devices = size_x * size_y
    me = lax.axis_index("tx") * size_y + lax.axis_index("ty")
    barrier = pltpu.get_barrier_semaphore()

    def greet(j, carry):
        to = lax.rem(me + j, devices)
        pl.semaphore_signal(
            barrier, inc=1, device_id=(to // size_y, lax.rem(to, size_y)), device_id_type=pl.DeviceIdType.MESH
        )
        return carry

    lax.fori_loop(1, devices, greet, 0)
    pl.semaphore_wait(barrier, devices - 1)

    def send(stage, source, target, to):
        pltpu.make_async_remote_copy(
            src_ref=source, dst_ref=target, send_sem=send_sem.at[stage], recv_sem=recv_sem.at[stage],
            device_id=(to // size_y, lax.rem(to, size_y)), device_id_type=pl.DeviceIdType.MESH,
        ).start()

    def wait(ref, sem):
        pltpu.make_async_copy(ref, ref, sem).wait()

    return devices, me, send, wait


def fetch(sem, *pairs):
    loads = [pltpu.make_async_copy(source, target, sem.at[k]) for k, (source, target) in enumerate(pairs)]
    for load in loads:
        load.start()
    return loads


def transform_kernel(
    size_x, size_y, own, half, total,
    turned_ref, first_hbm, twist_hbm, second_hbm, alpha_hbm, mix_hbm, swap_hbm,
    table_ref, value_ref, column_ref, high_ref, low_ref, pass_ref, beta_ref,
    first_ref, twist_ref, second_ref, alpha_ref, mix_ref, swap_ref,
    send_sem, recv_sem, load_sem,
):
    devices, me, send, wait = meet(size_x, size_y, send_sem, recv_sem)
    others = devices - 1
    high_rows = 2 * own
    span = 2 * half * high_rows

    def send_columns(j, carry):
        to = lax.rem(me + j, devices)
        send(0, turned_ref.at[to], column_ref.at[me], to)
        return carry

    lax.fori_loop(1, devices, send_columns, 0)
    loads = fetch(
        load_sem, (turned_ref.at[me], column_ref.at[me]),
        (first_hbm, first_ref), (twist_hbm, twist_ref), (second_hbm, second_ref),
        (alpha_hbm, alpha_ref), (mix_hbm, mix_ref), (swap_hbm, swap_ref),
    )
    for load in loads:
        load.wait()
    wait(column_ref.at[pl.ds(0, others)], recv_sem.at[0])
    for c in range(own):
        high, low = split(column_ref[:, c].reshape(RAD, RAD))
        high_ref[:, c * RAD : (c + 1) * RAD] = high
        low_ref[:, c * RAD : (c + 1) * RAD] = low

    group = first_ref.shape[0]
    height = half * 8

    def transform(b, carry):
        at = lax.rem(b + me // 8, group)
        section = product((first_ref[at, 0], first_ref[at, 1]), (high_ref[...], low_ref[...]))
        twist_cos, twist_sin = twist_ref[at, 0], twist_ref[at, 1]
        turned = []
        for c in range(own):
            real = section[: 2 * height, c * RAD : (c + 1) * RAD]
            imag = section[2 * height :, c * RAD : (c + 1) * RAD]
            turned.append(
                jnp.concatenate([real * twist_cos + imag * twist_sin, imag * twist_cos - real * twist_sin], axis=1)
            )
        for h in range(2):
            left = jnp.concatenate([part[h * height : (h + 1) * height] for part in turned], axis=0)
            bins = product(split(left), (second_ref[0, h], second_ref[1, h]))
            for c in range(own):
                for i in range(half):
                    row = c * height + i * 8
                    for side in range(2):
                        tile = (2 * i + side) * high_rows
                        pass_ref[pl.ds(at * 8 * span + tile + h * own + c, 8, stride=span), :] = bins[
                            row : row + 8, side * 128 : side * 128 + 128
                        ]
        for j in range(8):
            to = at * 8 + lax.rem(me + j, 8)

            @pl.when(to != me)
            def _():
                part = lambda ref, k: ref.at[pl.ds(pl.multiple_of(k * span, span), span)]
                send(1, part(pass_ref, to), part(value_ref, me), to)

        return carry

    lax.fori_loop(0, group, transform, 0)
    mine = pl.ds(pl.multiple_of(me * span, span), span)
    value_ref[mine, :] = pass_ref[mine, :]

    count = alpha_ref.shape[1]
    cols = count // 2
    row = lax.broadcasted_iota(jnp.int32, (count, 128), 0)
    lane = lax.broadcasted_iota(jnp.int32, (count, 128), 1)
    at = jnp.where(me == 0, jnp.where(lane == half, RAD // 2, devices * lane), me + 2 * devices * lane)
    angle = (row // high_rows * own + row % own) * at
    angle = angle.astype(jnp.float32) * (two_pi / total)
    beta_ref[0] = jnp.cos(angle)
    beta_ref[1] = jnp.where(row // own % 2 == 1, -1.0, 1.0) * jnp.sin(angle)
    wait(value_ref.at[pl.ds(0, others * span)], recv_sem.at[1])

    is_upper = lax.broadcasted_iota(jnp.int32, (count, RAD), 0) // own % 2 == 1

    def exchange_rows(block):
        cut = block.reshape(count // (2 * own), 2, own, RAD)
        return jnp.concatenate([cut[:, 1:], cut[:, :1]], axis=1).reshape(count, RAD)

    def twist(block, at):
        beta_cos, beta_sin = beta_ref[0, :, at : at + 1], beta_ref[1, :, at : at + 1]
        theta_cos = alpha_ref[0] * beta_cos - alpha_ref[1] * beta_sin
        theta_sin = alpha_ref[1] * beta_cos + alpha_ref[0] * beta_sin
        return theta_cos * block + theta_sin * exchange_rows(block)

    mix = mix_ref[0], mix_ref[1]

    def values(i):
        part = value_ref[...].reshape(devices, 2 * half, high_rows, 128)
        return jnp.concatenate([part[:, 2 * i + side].reshape(count, 128) for side in range(2)], axis=1)

    def put(result, h, i):
        for side in range(2):
            at = pl.ds(8 * side + h * half + i, cols, stride=16)
            table_ref[at, :] = result[:, side * 128 : (side + 1) * 128]

    for i in range(half):
        result = product(mix, split(twist(values(i), i)))
        for h in range(2):
            put(result[h * cols : (h + 1) * cols], h, i)

    @pl.when(me == 0)
    def _():
        block = values(0)
        high, low = split(block)
        for h in range(2):
            turn = lambda part: jnp.dot(part, swap_ref[h], preferred_element_type=jnp.float32)
            mirror = exchange_rows(turn(high) + turn(low))
            keep = is_upper if h else ~is_upper
            spun = split(twist(jnp.where(keep, block, mirror), h * half))
            rows_of = slice(h * cols, (h + 1) * cols)
            put(product((mix_ref[0, rows_of], mix_ref[1, rows_of]), spun), h, 0)

    wait(turned_ref.at[pl.ds(0, others)], send_sem.at[0])
    wait(pass_ref.at[pl.ds(0, others * span)], send_sem.at[1])


def deliver_kernel(
    size_x, size_y, half, total,
    start_ref, width_ref, gains_ref, slot_ref, table_ref, place_hbm, inner_hbm, twist_hbm, outer_hbm, when_hbm,
    out_ref, leave_ref, land_ref, gain_ref, phase_ref, place_ref, inner_ref, twist_ref, outer_ref, when_ref,
    send_sem, recv_sem, load_sem,
):
    devices, me, send, wait = meet(size_x, size_y, send_sem, recv_sem)
    pairs, height = leave_ref.shape[1:3]
    rows = total // RAD
    loads = fetch(
        load_sem, (place_hbm, place_ref), (when_hbm, when_ref), (inner_hbm, inner_ref), (twist_hbm, twist_ref),
        (outer_hbm, outer_ref),
    )
    shape = (2 * half, 128)
    lane = lax.broadcasted_iota(jnp.int32, shape, 1)
    is_low = lane < VL
    is_back = lax.broadcasted_iota(jnp.int32, shape, 0) >= half
    row = lax.broadcasted_iota(jnp.int32, shape, 0)
    index = jnp.where(is_back, row - half, row)
    residue = jnp.where(me == 0, devices * index, me + 2 * devices * index)
    residue = jnp.where((me == 0) & (row == half), RAD // 2, residue)
    residue = jnp.where(is_back, RAD - residue, residue)

    def load(tile):
        return table_ref[tile][: 2 * half]

    def window(slot):
        start = start_ref[jnp.maximum(slot_ref[slot], 0)]
        block = start // BL
        back = rows // VL - 2 - block
        tiles_of = [block // 2, (block + 1) // 2, back // 2, (back + 1) // 2]
        ahead_high, ahead_low, back_high, back_low = [load(t) for t in tiles_of]
        picked = jnp.where(is_low, jnp.where(is_back, back_low, ahead_low), jnp.where(is_back, back_high, ahead_high))
        ahead_at = 128 * jnp.where(is_low, tiles_of[1], tiles_of[0]) + lane
        back_at = rows - 1 - (128 * jnp.where(is_low, tiles_of[3], tiles_of[2]) + lane)
        place = RAD * jnp.where(is_back, back_at, ahead_at) + residue - start
        picked = jnp.where((place >= 0) & (place < BL), picked, 0.0)
        return picked + pltpu.roll(picked, VL, 1)

    def step(j, carry):
        to = lax.rem(me + j, devices)
        for k in range(pairs):
            slot = 2 * (to * pairs + k)
            leave_ref[to, k] = jnp.where(is_low, window(slot), window(slot + 1))

        @pl.when(to != me)
        def _():
            send(0, leave_ref.at[to], land_ref.at[me], to)

        return carry

    lax.fori_loop(1, devices + 1, step, 0)
    land_ref[me] = leave_ref[me]
    for load in loads:
        load.wait()

    is_low = lax.broadcasted_iota(jnp.int32, (1, 128), 1) < VL
    for p in range(pairs):
        slots = [slot_ref[(me * pairs + p) * 2 + k] for k in range(2)]
        of = lambda ref: jnp.where(is_low, *[ref[jnp.maximum(slot, 0)] for slot in slots])
        shift = of(start_ref) & (BL - 1)
        width = of(width_ref)
        rate = two_pi / width.astype(jnp.float32)
        scale = jnp.where(jnp.where(is_low, *slots) >= 0, of(gains_ref) / jnp.sqrt(width.astype(jnp.float32)), 0.0)
        position = (place_ref[...] - shift) & (BL - 1)
        turn = (position.astype(jnp.float32) + 0.5) * rate
        gain_ref[p] = jnp.where(position < width, 0.5 - 0.5 * jnp.cos(turn), 0.0)
        angle = ((when_ref[...] * shift) & (BL - 1)).astype(jnp.float32) * (two_pi / BL)
        phase_cos, phase_sin = jnp.cos(angle), jnp.sin(angle)
        phase_ref[p, 0] = (phase_cos - phase_sin) * scale
        phase_ref[p, 1] = (phase_cos + phase_sin) * scale

    wait(land_ref.at[pl.ds(0, devices - 1)], recv_sem.at[0])
    is_back = lax.broadcasted_iota(jnp.int32, (RAD, 1), 0) % height >= height // 2
    stacked = []
    for p in range(pairs):
        tapered = land_ref[:, p].reshape(RAD, 128) * gain_ref[p]
        part = product(split(tapered), (inner_ref[0], inner_ref[1]))
        part = jnp.where(is_back, part[:, 256:], part[:, :256])
        real, imag = part[:, :128], part[:, 128:]
        twist_cos, twist_sin = twist_ref[0], twist_ref[1]
        stacked.append(
            jnp.concatenate([real * twist_cos + imag * twist_sin, imag * twist_cos - real * twist_sin], axis=0)
        )
    result = product((outer_ref[0], outer_ref[1]), split(jnp.concatenate(stacked, axis=1)))
    for p in range(pairs):
        lanes = slice(p * 128, (p + 1) * 128)
        out_ref[p] = result[:RAD, lanes] * phase_ref[p, 0] - result[RAD:, lanes] * phase_ref[p, 1]
    wait(leave_ref.at[pl.ds(0, devices - 1)], send_sem.at[0])


def spectrum(turned, bands, base, total):
    size_x, size_y = lax.axis_size("tx"), lax.axis_size("ty")
    devices, _, half = base.shape
    own = turned.shape[1]
    cols = devices * own
    count = 2 * cols
    span = np.arange(RAD)
    col = np.arange(cols)
    sign = np.array([1.0, -1.0])[None, :, None]

    def rows_of(angle):
        part = angle.reshape(devices, 1, own, -1)
        put = lambda array: np.broadcast_to(array, (devices, 2, own, part.shape[-1])).reshape(count, -1)
        return np.stack([put(np.cos(part)), put(sign[..., None] * np.sin(part))]).astype(np.float32)

    alpha = rows_of(grid(col, RAD * span, total))
    angle = grid(col, col, cols).reshape(cols, devices, 1, own)
    ahead = np.concatenate([np.cos(angle), np.sin(angle)], axis=2)
    back = np.concatenate([-np.sin(angle), np.cos(angle)], axis=2)
    mix = np.stack([ahead, back]).reshape(count, count)
    swap = np.zeros((2, RAD, RAD))
    swap[0, (-span) % RAD, span] = 1.0
    swap[1, RAD - 1 - span, span] = 1.0
    order = base.reshape(devices // 8, 8, 2, half).transpose(0, 2, 3, 1).reshape(devices // 8, -1)
    angle = grid(order.reshape(-1), span, RAD).reshape(order.shape + (RAD,))
    first = np.concatenate([np.cos(angle), -np.sin(angle)], axis=1)
    angle = grid(order.reshape(-1), span, RAD * RAD).reshape(order.shape + (RAD,))
    twist = np.stack([np.cos(angle), np.sin(angle)], axis=1)
    angle = grid(span, span, RAD)
    cos_m, sin_m = np.cos(angle), np.sin(angle)
    minus = np.concatenate([cos_m + sin_m, sin_m - cos_m], axis=0)
    plus = np.concatenate([cos_m - sin_m, cos_m + sin_m], axis=0)
    second = np.stack([minus, plus]) / math.sqrt(total)
    smem = pl.BlockSpec(memory_space=pltpu.SMEM)
    vmem = pl.BlockSpec(memory_space=pltpu.VMEM)
    rows = total // RAD
    pairs = bands[3].shape[0] // (2 * devices)
    shape = (devices, pairs, 2 * half, 128)
    f32, bf16 = jnp.float32, jnp.bfloat16
    hbm = pl.BlockSpec(memory_space=pl.ANY)
    first, twist, second = const_split(first).swapaxes(0, 1), const(twist), const_split(second)
    room = lambda *arrays: [pltpu.VMEM(array.shape, array.dtype) for array in arrays]
    sems = lambda n: [pltpu.SemaphoreType.DMA((n,)), pltpu.SemaphoreType.DMA((n,))]
    limit = 48 * 1024 * 1024
    remote = lambda k: pltpu.CompilerParams(vmem_limit_bytes=limit, collective_id=k, has_side_effects=True)
    alpha, mix = const(alpha), const_split(mix)
    swap = jnp.asarray(swap.astype(np.float32).astype(bf16))
    table = pl.pallas_call(
        lambda *refs: transform_kernel(size_x, size_y, own, half, total, *refs),
        out_shape=jax.ShapeDtypeStruct((rows // 16, 128), f32),
        in_specs=[hbm] * 7,
        out_specs=vmem,
        scratch_shapes=[
            pltpu.VMEM((count * half * 2, 128), f32),
            pltpu.VMEM(turned.shape, f32),
            pltpu.VMEM((RAD, own * RAD), bf16),
            pltpu.VMEM((RAD, own * RAD), bf16),
            pltpu.VMEM((count * half * 2, 128), f32),
            pltpu.VMEM((2, count, 128), f32),
        ] + room(first, twist, second, alpha, mix, swap) + sems(2) + [pltpu.SemaphoreType.DMA((7,))],
        compiler_params=remote(0),
        name="transform",
    )(turned, first, twist, second, alpha, mix, swap)
    table = table.reshape(rows // 128, 8, 128)

    all_residue = (base * np.array([1, -1])[None, :, None]) % RAD
    lane = np.arange(VL)
    back = np.stack([lane, VL - 1 - lane])
    place = back[None, :, None, :] * RAD + all_residue[..., None]
    place = jnp.asarray(np.tile(place.reshape(RAD, VL), (1, 2)).astype(np.int32))
    angle = np.stack([grid(back[0], lane, VL), grid(back[1], lane, VL)])
    both = np.stack([np.cos(angle), -np.sin(angle)])
    inner = const_split(np.einsum("bd,chvt->bvhcdt", np.eye(2), both).reshape(2 * VL, 8 * VL))
    angle = np.tile(grid(all_residue.reshape(-1), lane, BL), (1, 2))
    spin = const(np.stack([np.cos(angle), np.sin(angle)]))
    angle = grid(span, all_residue.reshape(-1), RAD)
    cos_m, sin_m = np.cos(angle), np.sin(angle)
    outer = const_split(np.block([[cos_m, sin_m], [-sin_m, cos_m]]))
    when = jnp.asarray(np.tile(np.arange(BL).reshape(RAD, VL), (1, 2)).astype(np.int32))
    return pl.pallas_call(
        lambda *refs: deliver_kernel(size_x, size_y, half, total, *refs),
        out_shape=jax.ShapeDtypeStruct((pairs, RAD, 128), f32),
        in_specs=[smem] * 4 + [vmem] + [hbm] * 5,
        out_specs=vmem,
        scratch_shapes=[
            pltpu.VMEM(shape, f32),
            pltpu.VMEM(shape, f32),
            pltpu.VMEM((pairs, RAD, 128), f32),
            pltpu.VMEM((pairs, 2, RAD, 128), f32),
        ] + room(place, inner, spin, outer, when) + sems(1) + [pltpu.SemaphoreType.DMA((5,))],
        compiler_params=remote(1),
        name="deliver",
    )(*bands, table, place, inner, spin, outer, when)


def body(signal, band_start, band_width, band_gain, slot_band):
    devices = lax.axis_size("tx") * lax.axis_size("ty")
    length = signal.shape[0]
    total = length * devices
    own = length // (RAD * RAD)
    cols = own * devices
    chunk = length // cols
    base = row_bases(devices)
    half = base.shape[2]

    turned = signal.reshape(chunk // RAD, RAD, cols).transpose(2, 0, 1)
    turned = turned.reshape(devices, own, chunk // RAD, RAD)
    slots = slot_band.shape[0] // devices
    result = spectrum(turned, (band_start, band_width, band_gain, slot_band), base, total)
    result = result.reshape(slots // 2, RAD, 2, VL).transpose(0, 2, 1, 3)
    return result.reshape(slots, BL)


def solution(mesh):
    return jax.shard_map(
        body,
        mesh=mesh,
        in_specs=(P(AXES), P(), P(), P(), P()),
        out_specs=P(AXES, None),
        check_vma=False,
    )
```

```python
import math

import jax
import jax.numpy as jnp
import numpy as np
from jax import lax
from jax.experimental import pallas as pl
from jax.experimental.pallas import tpu as pltpu
from jax.sharding import PartitionSpec as P

BL = 16384
RAD = 256
VL = BL // RAD

two_pi = 2.0 * math.pi
AXES = ("tx", "ty")


def grid(first, second, modulus):
    return (two_pi / modulus) * (np.outer(first, second) % modulus)


def const(array):
    return jnp.asarray(np.ascontiguousarray(array, dtype=np.float32))


def row_bases(devices):
    half = RAD // (2 * devices)
    base = np.zeros((devices, 2, half), np.int64)
    for f in range(devices):
        for i in range(half):
            base[f, :, i] = f + 2 * devices * i if f else devices * i
    base[0, 1, 0] = RAD // 2
    return base


def split(array):
    high = array.astype(jnp.bfloat16)
    return high, (array - high.astype(jnp.float32)).astype(jnp.bfloat16)


def const_split(array):
    array = np.ascontiguousarray(array, dtype=np.float32)
    high = array.astype(jnp.bfloat16)
    return jnp.asarray(np.stack([high, (array - high.astype(np.float32)).astype(jnp.bfloat16)]))


def product(left, right):
    (left_high, left_low), (right_high, right_low) = left, right
    one = lambda a, b: jnp.dot(a, b, preferred_element_type=jnp.float32)
    return one(left_high, right_high) + (one(left_high, right_low) + one(left_low, right_high))


def meet(size_x, size_y, send_sem, recv_sem):
    devices = size_x * size_y
    me = lax.axis_index("tx") * size_y + lax.axis_index("ty")
    barrier = pltpu.get_barrier_semaphore()

    def greet(j, carry):
        to = lax.rem(me + j, devices)
        pl.semaphore_signal(
            barrier, inc=1, device_id=(to // size_y, lax.rem(to, size_y)), device_id_type=pl.DeviceIdType.MESH
        )
        return carry

    lax.fori_loop(1, devices, greet, 0)
    pl.semaphore_wait(barrier, devices - 1)

    def send(stage, source, target, to):
        pltpu.make_async_remote_copy(
            src_ref=source, dst_ref=target, send_sem=send_sem.at[stage], recv_sem=recv_sem.at[stage],
            device_id=(to // size_y, lax.rem(to, size_y)), device_id_type=pl.DeviceIdType.MESH,
        ).start()

    def wait(ref, sem):
        pltpu.make_async_copy(ref, ref, sem).wait()

    return devices, me, send, wait


def fetch(sem, *pairs):
    loads = [pltpu.make_async_copy(source, target, sem.at[k]) for k, (source, target) in enumerate(pairs)]
    for load in loads:
        load.start()
    return loads


def transform_kernel(
    size_x, size_y, own, half, total,
    turned_ref, first_hbm, twist_hbm, second_hbm, alpha_hbm, mix_hbm, swap_hbm,
    table_ref, value_ref, column_ref, high_ref, low_ref, pass_ref, beta_ref,
    first_ref, twist_ref, second_ref, alpha_ref, mix_ref, swap_ref,
    send_sem, recv_sem, load_sem,
):
    devices, me, send, wait = meet(size_x, size_y, send_sem, recv_sem)
    others = devices - 1
    high_rows = 2 * own
    span = 2 * half * high_rows

    def send_columns(j, carry):
        step = lax.rem(j, 2) * (size_y // 2) + lax.rem(j, size_y) // 2
        across = lax.rem(me // size_y + j // size_y, size_x)
        to = across * size_y + lax.rem(me + step, size_y)
        send(0, turned_ref.at[to], column_ref.at[me], to)
        return carry

    lax.fori_loop(1, devices, send_columns, 0)
    loads = fetch(
        load_sem, (turned_ref.at[me], column_ref.at[me]),
        (first_hbm, first_ref), (twist_hbm, twist_ref), (second_hbm, second_ref),
        (alpha_hbm, alpha_ref), (mix_hbm, mix_ref), (swap_hbm, swap_ref),
    )
    for load in loads:
        load.wait()
    wait(column_ref.at[pl.ds(0, others)], recv_sem.at[0])
    for c in range(own):
        high, low = split(column_ref[:, c].reshape(RAD, RAD))
        high_ref[:, c * RAD : (c + 1) * RAD] = high
        low_ref[:, c * RAD : (c + 1) * RAD] = low

    group = first_ref.shape[0]
    height = half * 8

    def transform(b, carry):
        at = lax.rem(b + me // 8, group)
        section = product((first_ref[at, 0], first_ref[at, 1]), (high_ref[...], low_ref[...]))
        twist_cos, twist_sin = twist_ref[at, 0], twist_ref[at, 1]
        turned = []
        for c in range(own):
            real = section[: 2 * height, c * RAD : (c + 1) * RAD]
            imag = section[2 * height :, c * RAD : (c + 1) * RAD]
            turned.append(
                jnp.concatenate([real * twist_cos + imag * twist_sin, imag * twist_cos - real * twist_sin], axis=1)
            )
        for h in range(2):
            left = jnp.concatenate([part[h * height : (h + 1) * height] for part in turned], axis=0)
            bins = product(split(left), (second_ref[0, h], second_ref[1, h]))
            for c in range(own):
                for i in range(half):
                    row = c * height + i * 8
                    for side in range(2):
                        tile = (2 * i + side) * high_rows
                        pass_ref[pl.ds(at * 8 * span + tile + h * own + c, 8, stride=span), :] = bins[
                            row : row + 8, side * 128 : side * 128 + 128
                        ]
        for j in range(8):
            to = at * 8 + lax.rem(me + j % 2 * 4 + j // 2, 8)

            @pl.when(to != me)
            def _():
                part = lambda ref, k: ref.at[pl.ds(pl.multiple_of(k * span, span), span)]
                send(1, part(pass_ref, to), part(value_ref, me), to)

        return carry

    lax.fori_loop(0, group, transform, 0)
    mine = pl.ds(pl.multiple_of(me * span, span), span)
    value_ref[mine, :] = pass_ref[mine, :]

    count = alpha_ref.shape[1]
    cols = count // 2
    row = lax.broadcasted_iota(jnp.int32, (count, 128), 0)
    lane = lax.broadcasted_iota(jnp.int32, (count, 128), 1)
    at = jnp.where(me == 0, jnp.where(lane == half, RAD // 2, devices * lane), me + 2 * devices * lane)
    angle = (row // high_rows * own + row % own) * at
    angle = angle.astype(jnp.float32) * (two_pi / total)
    beta_ref[0] = jnp.cos(angle)
    beta_ref[1] = jnp.where(row // own % 2 == 1, -1.0, 1.0) * jnp.sin(angle)
    wait(value_ref.at[pl.ds(0, others * span)], recv_sem.at[1])

    is_upper = lax.broadcasted_iota(jnp.int32, (count, RAD), 0) // own % 2 == 1

    def exchange_rows(block):
        cut = block.reshape(count // (2 * own), 2, own, RAD)
        return jnp.concatenate([cut[:, 1:], cut[:, :1]], axis=1).reshape(count, RAD)

    def twist(block, at):
        beta_cos, beta_sin = beta_ref[0, :, at : at + 1], beta_ref[1, :, at : at + 1]
        theta_cos = alpha_ref[0] * beta_cos - alpha_ref[1] * beta_sin
        theta_sin = alpha_ref[1] * beta_cos + alpha_ref[0] * beta_sin
        return theta_cos * block + theta_sin * exchange_rows(block)

    mix = mix_ref[0], mix_ref[1]

    def values(i):
        part = value_ref[...].reshape(devices, 2 * half, high_rows, 128)
        return jnp.concatenate([part[:, 2 * i + side].reshape(count, 128) for side in range(2)], axis=1)

    def put(result, h, i):
        for side in range(2):
            at = pl.ds(8 * side + h * half + i, cols, stride=16)
            table_ref[at, :] = result[:, side * 128 : (side + 1) * 128]

    def general(i):
        result = product(mix, split(twist(values(i), i)))
        for h in range(2):
            put(result[h * cols : (h + 1) * cols], h, i)

    for i in range(1, half):
        general(i)

    @pl.when(me != 0)
    def _():
        general(0)

    @pl.when(me == 0)
    def _():
        block = values(0)
        high, low = split(block)
        for h in range(2):
            turn = lambda part: jnp.dot(part, swap_ref[h], preferred_element_type=jnp.float32)
            mirror = exchange_rows(turn(high) + turn(low))
            keep = is_upper if h else ~is_upper
            spun = split(twist(jnp.where(keep, block, mirror), h * half))
            rows_of = slice(h * cols, (h + 1) * cols)
            put(product((mix_ref[0, rows_of], mix_ref[1, rows_of]), spun), h, 0)

    wait(turned_ref.at[pl.ds(0, others)], send_sem.at[0])
    wait(pass_ref.at[pl.ds(0, others * span)], send_sem.at[1])


def deliver_kernel(
    size_x, size_y, half, total,
    start_ref, width_ref, gains_ref, slot_ref, table_ref, place_hbm, inner_hbm, twist_hbm, outer_hbm, when_hbm,
    out_ref, leave_ref, land_ref, gain_ref, phase_ref, place_ref, inner_ref, twist_ref, outer_ref, when_ref,
    send_sem, recv_sem, load_sem,
):
    devices, me, send, wait = meet(size_x, size_y, send_sem, recv_sem)
    pairs, height = leave_ref.shape[1:3]
    rows = total // RAD
    loads = fetch(
        load_sem, (place_hbm, place_ref), (when_hbm, when_ref), (inner_hbm, inner_ref), (twist_hbm, twist_ref),
        (outer_hbm, outer_ref),
    )
    shape = (2 * half, 128)
    lane = lax.broadcasted_iota(jnp.int32, shape, 1)
    is_low = lane < VL
    is_back = lax.broadcasted_iota(jnp.int32, shape, 0) >= half
    row = lax.broadcasted_iota(jnp.int32, shape, 0)
    index = jnp.where(is_back, row - half, row)
    residue = jnp.where(me == 0, devices * index, me + 2 * devices * index)
    residue = jnp.where((me == 0) & (row == half), RAD // 2, residue)
    residue = jnp.where(is_back, RAD - residue, residue)

    def load(tile):
        return table_ref[tile][: 2 * half]

    def window(slot):
        start = start_ref[jnp.maximum(slot_ref[slot], 0)]
        block = start // BL
        back = rows // VL - 2 - block
        tiles_of = [block // 2, (block + 1) // 2, back // 2, (back + 1) // 2]
        ahead_high, ahead_low, back_high, back_low = [load(t) for t in tiles_of]
        picked = jnp.where(is_low, jnp.where(is_back, back_low, ahead_low), jnp.where(is_back, back_high, ahead_high))
        ahead_at = 128 * jnp.where(is_low, tiles_of[1], tiles_of[0]) + lane
        back_at = rows - 1 - (128 * jnp.where(is_low, tiles_of[3], tiles_of[2]) + lane)
        place = RAD * jnp.where(is_back, back_at, ahead_at) + residue - start
        picked = jnp.where((place >= 0) & (place < BL), picked, 0.0)
        return picked + pltpu.roll(picked, VL, 1)

    def step(j, carry):
        to = lax.rem(me + j, devices)
        for k in range(pairs):
            slot = 2 * (to * pairs + k)
            leave_ref[to, k] = jnp.where(is_low, window(slot), window(slot + 1))

        @pl.when(to != me)
        def _():
            send(0, leave_ref.at[to], land_ref.at[me], to)

        return carry

    lax.fori_loop(1, devices + 1, step, 0)
    land_ref[me] = leave_ref[me]
    for load in loads:
        load.wait()

    is_low = lax.broadcasted_iota(jnp.int32, (1, 128), 1) < VL
    for p in range(pairs):
        slots = [slot_ref[(me * pairs + p) * 2 + k] for k in range(2)]
        of = lambda ref: jnp.where(is_low, *[ref[jnp.maximum(slot, 0)] for slot in slots])
        shift = of(start_ref) & (BL - 1)
        width = of(width_ref)
        rate = two_pi / width.astype(jnp.float32)
        scale = jnp.where(jnp.where(is_low, *slots) >= 0, of(gains_ref) / jnp.sqrt(width.astype(jnp.float32)), 0.0)
        position = (place_ref[...] - shift) & (BL - 1)
        turn = (position.astype(jnp.float32) + 0.5) * rate
        gain_ref[p] = jnp.where(position < width, 0.5 - 0.5 * jnp.cos(turn), 0.0)
        angle = ((when_ref[...] * shift) & (BL - 1)).astype(jnp.float32) * (two_pi / BL)
        phase_cos, phase_sin = jnp.cos(angle), jnp.sin(angle)
        phase_ref[p, 0] = (phase_cos - phase_sin) * scale
        phase_ref[p, 1] = (phase_cos + phase_sin) * scale

    wait(land_ref.at[pl.ds(0, devices - 1)], recv_sem.at[0])
    is_back = lax.broadcasted_iota(jnp.int32, (RAD, 1), 0) % height >= height // 2
    stacked = []
    for p in range(pairs):
        tapered = land_ref[:, p].reshape(RAD, 128) * gain_ref[p]
        part = product(split(tapered), (inner_ref[0], inner_ref[1]))
        part = jnp.where(is_back, part[:, 256:], part[:, :256])
        real, imag = part[:, :128], part[:, 128:]
        twist_cos, twist_sin = twist_ref[0], twist_ref[1]
        stacked.append(
            jnp.concatenate([real * twist_cos + imag * twist_sin, imag * twist_cos - real * twist_sin], axis=0)
        )
    result = product((outer_ref[0], outer_ref[1]), split(jnp.concatenate(stacked, axis=1)))
    for p in range(pairs):
        lanes = slice(p * 128, (p + 1) * 128)
        out_ref[p] = result[:RAD, lanes] * phase_ref[p, 0] - result[RAD:, lanes] * phase_ref[p, 1]
    wait(leave_ref.at[pl.ds(0, devices - 1)], send_sem.at[0])


def spectrum(turned, bands, base, total):
    size_x, size_y = lax.axis_size("tx"), lax.axis_size("ty")
    devices, _, half = base.shape
    own = turned.shape[1]
    cols = devices * own
    count = 2 * cols
    span = np.arange(RAD)
    col = np.arange(cols)
    sign = np.array([1.0, -1.0])[None, :, None]

    def rows_of(angle):
        part = angle.reshape(devices, 1, own, -1)
        put = lambda array: np.broadcast_to(array, (devices, 2, own, part.shape[-1])).reshape(count, -1)
        return np.stack([put(np.cos(part)), put(sign[..., None] * np.sin(part))]).astype(np.float32)

    alpha = rows_of(grid(col, RAD * span, total))
    angle = grid(col, col, cols).reshape(cols, devices, 1, own)
    ahead = np.concatenate([np.cos(angle), np.sin(angle)], axis=2)
    back = np.concatenate([-np.sin(angle), np.cos(angle)], axis=2)
    mix = np.stack([ahead, back]).reshape(count, count)
    swap = np.zeros((2, RAD, RAD))
    swap[0, (-span) % RAD, span] = 1.0
    swap[1, RAD - 1 - span, span] = 1.0
    order = base.reshape(devices // 8, 8, 2, half).transpose(0, 2, 3, 1).reshape(devices // 8, -1)
    angle = grid(order.reshape(-1), span, RAD).reshape(order.shape + (RAD,))
    first = np.concatenate([np.cos(angle), -np.sin(angle)], axis=1)
    angle = grid(order.reshape(-1), span, RAD * RAD).reshape(order.shape + (RAD,))
    twist = np.stack([np.cos(angle), np.sin(angle)], axis=1)
    angle = grid(span, span, RAD)
    cos_m, sin_m = np.cos(angle), np.sin(angle)
    minus = np.concatenate([cos_m + sin_m, sin_m - cos_m], axis=0)
    plus = np.concatenate([cos_m - sin_m, cos_m + sin_m], axis=0)
    second = np.stack([minus, plus]) / math.sqrt(total)
    smem = pl.BlockSpec(memory_space=pltpu.SMEM)
    vmem = pl.BlockSpec(memory_space=pltpu.VMEM)
    rows = total // RAD
    pairs = bands[3].shape[0] // (2 * devices)
    shape = (devices, pairs, 2 * half, 128)
    f32, bf16 = jnp.float32, jnp.bfloat16
    hbm = pl.BlockSpec(memory_space=pl.ANY)
    first, twist, second = const_split(first).swapaxes(0, 1), const(twist), const_split(second)
    room = lambda *arrays: [pltpu.VMEM(array.shape, array.dtype) for array in arrays]
    sems = lambda n: [pltpu.SemaphoreType.DMA((n,)), pltpu.SemaphoreType.DMA((n,))]
    mib = 1024 * 1024
    remote = lambda k, limit: pltpu.CompilerParams(vmem_limit_bytes=limit, collective_id=k, has_side_effects=True)
    alpha, mix = const(alpha), const_split(mix)
    swap = jnp.asarray(swap.astype(np.float32).astype(bf16))
    table = pl.pallas_call(
        lambda *refs: transform_kernel(size_x, size_y, own, half, total, *refs),
        out_shape=jax.ShapeDtypeStruct((rows // 16, 128), f32),
        in_specs=[hbm] * 7,
        out_specs=vmem,
        scratch_shapes=[
            pltpu.VMEM((count * half * 2, 128), f32),
            pltpu.VMEM(turned.shape, f32),
            pltpu.VMEM((RAD, own * RAD), bf16),
            pltpu.VMEM((RAD, own * RAD), bf16),
            pltpu.VMEM((count * half * 2, 128), f32),
            pltpu.VMEM((2, count, 128), f32),
        ] + room(first, twist, second, alpha, mix, swap) + sems(2) + [pltpu.SemaphoreType.DMA((7,))],
        compiler_params=remote(0, 60 * mib),
        name="transform",
    )(turned, first, twist, second, alpha, mix, swap)
    table = table.reshape(rows // 128, 8, 128)

    all_residue = (base * np.array([1, -1])[None, :, None]) % RAD
    lane = np.arange(VL)
    back = np.stack([lane, VL - 1 - lane])
    place = back[None, :, None, :] * RAD + all_residue[..., None]
    place = jnp.asarray(np.tile(place.reshape(RAD, VL), (1, 2)).astype(np.int32))
    angle = np.stack([grid(back[0], lane, VL), grid(back[1], lane, VL)])
    both = np.stack([np.cos(angle), -np.sin(angle)])
    inner = const_split(np.einsum("bd,chvt->bvhcdt", np.eye(2), both).reshape(2 * VL, 8 * VL))
    angle = np.tile(grid(all_residue.reshape(-1), lane, BL), (1, 2))
    spin = const(np.stack([np.cos(angle), np.sin(angle)]))
    angle = grid(span, all_residue.reshape(-1), RAD)
    cos_m, sin_m = np.cos(angle), np.sin(angle)
    outer = const_split(np.block([[cos_m, sin_m], [-sin_m, cos_m]]))
    when = jnp.asarray(np.tile(np.arange(BL).reshape(RAD, VL), (1, 2)).astype(np.int32))
    return pl.pallas_call(
        lambda *refs: deliver_kernel(size_x, size_y, half, total, *refs),
        out_shape=jax.ShapeDtypeStruct((pairs, RAD, 128), f32),
        in_specs=[smem] * 4 + [vmem] + [hbm] * 5,
        out_specs=vmem,
        scratch_shapes=[
            pltpu.VMEM(shape, f32),
            pltpu.VMEM(shape, f32),
            pltpu.VMEM((pairs, RAD, 128), f32),
            pltpu.VMEM((pairs, 2, RAD, 128), f32),
        ] + room(place, inner, spin, outer, when) + sems(1) + [pltpu.SemaphoreType.DMA((5,))],
        compiler_params=remote(1, 48 * mib),
        name="deliver",
    )(*bands, table, place, inner, spin, outer, when)


def body(signal, band_start, band_width, band_gain, slot_band):
    devices = lax.axis_size("tx") * lax.axis_size("ty")
    length = signal.shape[0]
    total = length * devices
    own = length // (RAD * RAD)
    cols = own * devices
    chunk = length // cols
    base = row_bases(devices)
    half = base.shape[2]

    turned = signal.reshape(chunk // RAD, RAD, cols).transpose(2, 0, 1)
    turned = turned.reshape(devices, own, chunk // RAD, RAD)
    slots = slot_band.shape[0] // devices
    result = spectrum(turned, (band_start, band_width, band_gain, slot_band), base, total)
    result = result.reshape(slots // 2, RAD, 2, VL).transpose(0, 2, 1, 3)
    return result.reshape(slots, BL)


def solution(mesh):
    return jax.shard_map(
        body,
        mesh=mesh,
        in_specs=(P(AXES), P(), P(), P(), P()),
        out_specs=P(AXES, None),
        check_vma=False,
    )
```

```python
import math

import jax
import jax.numpy as jnp
import numpy as np
from jax import lax
from jax.experimental import pallas as pl
from jax.experimental.pallas import tpu as pltpu
from jax.sharding import PartitionSpec as P

BL = 16384
RAD = 256
VL = BL // RAD

two_pi = 2.0 * math.pi
AXES = ("tx", "ty")


def grid(first, second, modulus):
    return (two_pi / modulus) * (np.outer(first, second) % modulus)


def const(array):
    return jnp.asarray(np.ascontiguousarray(array, dtype=np.float32))


def row_bases(devices):
    half = RAD // (2 * devices)
    base = np.zeros((devices, 2, half), np.int64)
    for f in range(devices):
        for i in range(half):
            base[f, :, i] = f + 2 * devices * i if f else devices * i
    base[0, 1, 0] = RAD // 2
    return base


def split(array):
    high = array.astype(jnp.bfloat16)
    return high, (array - high.astype(jnp.float32)).astype(jnp.bfloat16)


def const_split(array):
    array = np.ascontiguousarray(array, dtype=np.float32)
    high = array.astype(jnp.bfloat16)
    return jnp.asarray(np.stack([high, (array - high.astype(np.float32)).astype(jnp.bfloat16)]))


def product(left, right):
    (left_high, left_low), (right_high, right_low) = left, right
    one = lambda a, b: jnp.dot(a, b, preferred_element_type=jnp.float32)
    return one(left_high, right_high) + (one(left_high, right_low) + one(left_low, right_high))


def meet(size_x, size_y, send_sem, recv_sem):
    devices = size_x * size_y
    me = lax.axis_index("tx") * size_y + lax.axis_index("ty")
    barrier = pltpu.get_barrier_semaphore()

    def greet(j, carry):
        to = lax.rem(me + j, devices)
        pl.semaphore_signal(
            barrier, inc=1, device_id=(to // size_y, lax.rem(to, size_y)), device_id_type=pl.DeviceIdType.MESH
        )
        return carry

    lax.fori_loop(1, devices, greet, 0)
    pl.semaphore_wait(barrier, devices - 1)

    def send(stage, source, target, to):
        pltpu.make_async_remote_copy(
            src_ref=source, dst_ref=target, send_sem=send_sem.at[stage], recv_sem=recv_sem.at[stage],
            device_id=(to // size_y, lax.rem(to, size_y)), device_id_type=pl.DeviceIdType.MESH,
        ).start()

    def wait(ref, sem):
        pltpu.make_async_copy(ref, ref, sem).wait()

    return devices, me, send, wait


def fetch(sem, *pairs):
    loads = [pltpu.make_async_copy(source, target, sem.at[k]) for k, (source, target) in enumerate(pairs)]
    for load in loads:
        load.start()
    return loads


def transform_kernel(
    size_x, size_y, own, half, total,
    turned_ref, first_hbm, twist_hbm, second_hbm, alpha_hbm, mix_hbm, swap_hbm,
    table_ref, value_ref, column_ref, high_ref, low_ref, pass_ref, beta_ref,
    first_ref, twist_ref, second_ref, alpha_ref, mix_ref, swap_ref,
    send_sem, recv_sem, load_sem,
):
    devices, me, send, wait = meet(size_x, size_y, send_sem, recv_sem)
    others = devices - 1
    high_rows = 2 * own
    span = 2 * half * high_rows

    def send_columns(j, carry):
        to = lax.rem(me + j, devices)
        send(0, turned_ref.at[to], column_ref.at[me], to)
        return carry

    lax.fori_loop(1, devices, send_columns, 0)
    loads = fetch(
        load_sem, (turned_ref.at[me], column_ref.at[me]),
        (first_hbm, first_ref), (twist_hbm, twist_ref), (second_hbm, second_ref),
        (alpha_hbm, alpha_ref), (mix_hbm, mix_ref), (swap_hbm, swap_ref),
    )
    for load in loads:
        load.wait()
    wait(column_ref.at[pl.ds(0, others)], recv_sem.at[0])
    for c in range(own):
        high, low = split(column_ref[:, c].reshape(RAD, RAD))
        high_ref[:, c * RAD : (c + 1) * RAD] = high
        low_ref[:, c * RAD : (c + 1) * RAD] = low

    group = first_ref.shape[0]
    height = half * 8

    def transform(b, carry):
        at = lax.rem(b + me // 8, group)
        section = product((first_ref[at, 0], first_ref[at, 1]), (high_ref[...], low_ref[...]))
        twist_cos, twist_sin = twist_ref[at, 0], twist_ref[at, 1]
        turned = []
        for c in range(own):
            real = section[: 2 * height, c * RAD : (c + 1) * RAD]
            imag = section[2 * height :, c * RAD : (c + 1) * RAD]
            turned.append(
                jnp.concatenate([real * twist_cos + imag * twist_sin, imag * twist_cos - real * twist_sin], axis=1)
            )
        for h in range(2):
            left = jnp.concatenate([part[h * height : (h + 1) * height] for part in turned], axis=0)
            bins = product(split(left), (second_ref[0, h], second_ref[1, h]))
            for c in range(own):
                for i in range(half):
                    row = c * height + i * 8
                    for side in range(2):
                        tile = (2 * i + side) * high_rows
                        pass_ref[pl.ds(at * 8 * span + tile + h * own + c, 8, stride=span), :] = bins[
                            row : row + 8, side * 128 : side * 128 + 128
                        ]
        for j in range(8):
            to = at * 8 + lax.rem(me + j, 8)

            @pl.when(to != me)
            def _():
                part = lambda ref, k: ref.at[pl.ds(pl.multiple_of(k * span, span), span)]
                send(1, part(pass_ref, to), part(value_ref, me), to)

        return carry

    lax.fori_loop(0, group, transform, 0)
    mine = pl.ds(pl.multiple_of(me * span, span), span)
    value_ref[mine, :] = pass_ref[mine, :]

    count = alpha_ref.shape[1]
    cols = count // 2
    row = lax.broadcasted_iota(jnp.int32, (count, 128), 0)
    lane = lax.broadcasted_iota(jnp.int32, (count, 128), 1)
    at = jnp.where(me == 0, jnp.where(lane == half, RAD // 2, devices * lane), me + 2 * devices * lane)
    angle = (row // high_rows * own + row % own) * at
    angle = angle.astype(jnp.float32) * (two_pi / total)
    beta_ref[0] = jnp.cos(angle)
    beta_ref[1] = jnp.where(row // own % 2 == 1, -1.0, 1.0) * jnp.sin(angle)
    wait(value_ref.at[pl.ds(0, others * span)], recv_sem.at[1])

    is_upper = lax.broadcasted_iota(jnp.int32, (count, RAD), 0) // own % 2 == 1

    def exchange_rows(block):
        cut = block.reshape(count // (2 * own), 2, own, RAD)
        return jnp.concatenate([cut[:, 1:], cut[:, :1]], axis=1).reshape(count, RAD)

    def twist(block, at):
        beta_cos, beta_sin = beta_ref[0, :, at : at + 1], beta_ref[1, :, at : at + 1]
        theta_cos = alpha_ref[0] * beta_cos - alpha_ref[1] * beta_sin
        theta_sin = alpha_ref[1] * beta_cos + alpha_ref[0] * beta_sin
        return theta_cos * block + theta_sin * exchange_rows(block)

    mix = mix_ref[0], mix_ref[1]

    def values(i):
        part = value_ref[...].reshape(devices, 2 * half, high_rows, 128)
        return jnp.concatenate([part[:, 2 * i + side].reshape(count, 128) for side in range(2)], axis=1)

    def put(result, h, i):
        for side in range(2):
            at = pl.ds(8 * side + h * half + i, cols, stride=16)
            table_ref[at, :] = result[:, side * 128 : (side + 1) * 128]

    def general(i):
        result = product(mix, split(twist(values(i), i)))
        for h in range(2):
            put(result[h * cols : (h + 1) * cols], h, i)

    for i in range(1, half):
        general(i)

    @pl.when(me != 0)
    def _():
        general(0)

    @pl.when(me == 0)
    def _():
        block = values(0)
        high, low = split(block)
        for h in range(2):
            turn = lambda part: jnp.dot(part, swap_ref[h], preferred_element_type=jnp.float32)
            mirror = exchange_rows(turn(high) + turn(low))
            keep = is_upper if h else ~is_upper
            spun = split(twist(jnp.where(keep, block, mirror), h * half))
            rows_of = slice(h * cols, (h + 1) * cols)
            put(product((mix_ref[0, rows_of], mix_ref[1, rows_of]), spun), h, 0)

    wait(turned_ref.at[pl.ds(0, others)], send_sem.at[0])
    wait(pass_ref.at[pl.ds(0, others * span)], send_sem.at[1])


def deliver_kernel(
    size_x, size_y, half, total,
    start_ref, width_ref, gains_ref, slot_ref, table_hbm, place_hbm, inner_hbm, twist_hbm, outer_hbm, when_hbm,
    out_ref, leave_ref, land_ref, gain_ref, phase_ref, place_ref, inner_ref, twist_ref, outer_ref, when_ref,
    table_ref, send_sem, recv_sem, load_sem,
):
    loads = fetch(
        load_sem, (table_hbm, table_ref), (place_hbm, place_ref), (when_hbm, when_ref), (inner_hbm, inner_ref), (twist_hbm, twist_ref),
        (outer_hbm, outer_ref),
    )
    devices, me, send, wait = meet(size_x, size_y, send_sem, recv_sem)
    pairs, height = leave_ref.shape[1:3]
    rows = total // RAD
    shape = (2 * half, 128)
    lane = lax.broadcasted_iota(jnp.int32, shape, 1)
    is_low = lane < VL
    is_back = lax.broadcasted_iota(jnp.int32, shape, 0) >= half
    row = lax.broadcasted_iota(jnp.int32, shape, 0)
    index = jnp.where(is_back, row - half, row)
    residue = jnp.where(me == 0, devices * index, me + 2 * devices * index)
    residue = jnp.where((me == 0) & (row == half), RAD // 2, residue)
    residue = jnp.where(is_back, RAD - residue, residue)

    def load(tile):
        return table_ref[tile][: 2 * half]

    def window(slot):
        start = start_ref[jnp.maximum(slot_ref[slot], 0)]
        block = start // BL
        back = rows // VL - 2 - block
        tiles_of = [block // 2, (block + 1) // 2, back // 2, (back + 1) // 2]
        ahead_high, ahead_low, back_high, back_low = [load(t) for t in tiles_of]
        picked = jnp.where(is_low, jnp.where(is_back, back_low, ahead_low), jnp.where(is_back, back_high, ahead_high))
        ahead_at = 128 * jnp.where(is_low, tiles_of[1], tiles_of[0]) + lane
        back_at = rows - 1 - (128 * jnp.where(is_low, tiles_of[3], tiles_of[2]) + lane)
        place = RAD * jnp.where(is_back, back_at, ahead_at) + residue - start
        picked = jnp.where((place >= 0) & (place < BL), picked, 0.0)
        return picked + pltpu.roll(picked, VL, 1)

    def step(j, carry):
        to = lax.rem(me + j, devices)
        for k in range(pairs):
            slot = 2 * (to * pairs + k)
            leave_ref[to, k] = jnp.where(is_low, window(slot), window(slot + 1))

        @pl.when(to != me)
        def _():
            send(0, leave_ref.at[to], land_ref.at[me], to)

        return carry

    loads[0].wait()
    lax.fori_loop(1, devices + 1, step, 0)
    land_ref[me] = leave_ref[me]
    for copy in loads[1:]:
        copy.wait()

    is_low = lax.broadcasted_iota(jnp.int32, (1, 128), 1) < VL
    for p in range(pairs):
        slots = [slot_ref[(me * pairs + p) * 2 + k] for k in range(2)]
        of = lambda ref: jnp.where(is_low, *[ref[jnp.maximum(slot, 0)] for slot in slots])
        shift = of(start_ref) & (BL - 1)
        width = of(width_ref)
        rate = two_pi / width.astype(jnp.float32)
        scale = jnp.where(jnp.where(is_low, *slots) >= 0, of(gains_ref) / jnp.sqrt(width.astype(jnp.float32)), 0.0)
        position = (place_ref[...] - shift) & (BL - 1)
        turn = (position.astype(jnp.float32) + 0.5) * rate
        gain_ref[p] = jnp.where(position < width, 0.5 - 0.5 * jnp.cos(turn), 0.0)
        angle = ((when_ref[...] * shift) & (BL - 1)).astype(jnp.float32) * (two_pi / BL)
        phase_cos, phase_sin = jnp.cos(angle), jnp.sin(angle)
        phase_ref[p, 0] = (phase_cos - phase_sin) * scale
        phase_ref[p, 1] = (phase_cos + phase_sin) * scale

    wait(land_ref.at[pl.ds(0, devices - 1)], recv_sem.at[0])
    is_back = lax.broadcasted_iota(jnp.int32, (RAD, 1), 0) % height >= height // 2
    stacked = []
    for p in range(pairs):
        tapered = land_ref[:, p].reshape(RAD, 128) * gain_ref[p]
        part = product(split(tapered), (inner_ref[0], inner_ref[1]))
        part = jnp.where(is_back, part[:, 256:], part[:, :256])
        real, imag = part[:, :128], part[:, 128:]
        twist_cos, twist_sin = twist_ref[0], twist_ref[1]
        stacked.append(
            jnp.concatenate([real * twist_cos + imag * twist_sin, imag * twist_cos - real * twist_sin], axis=0)
        )
    result = product((outer_ref[0], outer_ref[1]), split(jnp.concatenate(stacked, axis=1)))
    for p in range(pairs):
        lanes = slice(p * 128, (p + 1) * 128)
        out_ref[p] = result[:RAD, lanes] * phase_ref[p, 0] - result[RAD:, lanes] * phase_ref[p, 1]
    wait(leave_ref.at[pl.ds(0, devices - 1)], send_sem.at[0])


def spectrum(turned, bands, base, total):
    size_x, size_y = lax.axis_size("tx"), lax.axis_size("ty")
    devices, _, half = base.shape
    own = turned.shape[1]
    cols = devices * own
    count = 2 * cols
    span = np.arange(RAD)
    col = np.arange(cols)
    sign = np.array([1.0, -1.0])[None, :, None]

    def rows_of(angle):
        part = angle.reshape(devices, 1, own, -1)
        put = lambda array: np.broadcast_to(array, (devices, 2, own, part.shape[-1])).reshape(count, -1)
        return np.stack([put(np.cos(part)), put(sign[..., None] * np.sin(part))]).astype(np.float32)

    alpha = rows_of(grid(col, RAD * span, total))
    angle = grid(col, col, cols).reshape(cols, devices, 1, own)
    ahead = np.concatenate([np.cos(angle), np.sin(angle)], axis=2)
    back = np.concatenate([-np.sin(angle), np.cos(angle)], axis=2)
    mix = np.stack([ahead, back]).reshape(count, count)
    swap = np.zeros((2, RAD, RAD))
    swap[0, (-span) % RAD, span] = 1.0
    swap[1, RAD - 1 - span, span] = 1.0
    order = base.reshape(devices // 8, 8, 2, half).transpose(0, 2, 3, 1).reshape(devices // 8, -1)
    angle = grid(order.reshape(-1), span, RAD).reshape(order.shape + (RAD,))
    first = np.concatenate([np.cos(angle), -np.sin(angle)], axis=1)
    angle = grid(order.reshape(-1), span, RAD * RAD).reshape(order.shape + (RAD,))
    twist = np.stack([np.cos(angle), np.sin(angle)], axis=1)
    angle = grid(span, span, RAD)
    cos_m, sin_m = np.cos(angle), np.sin(angle)
    minus = np.concatenate([cos_m + sin_m, sin_m - cos_m], axis=0)
    plus = np.concatenate([cos_m - sin_m, cos_m + sin_m], axis=0)
    second = np.stack([minus, plus]) / math.sqrt(total)
    smem = pl.BlockSpec(memory_space=pltpu.SMEM)
    vmem = pl.BlockSpec(memory_space=pltpu.VMEM)
    rows = total // RAD
    pairs = bands[3].shape[0] // (2 * devices)
    shape = (devices, pairs, 2 * half, 128)
    f32, bf16 = jnp.float32, jnp.bfloat16
    hbm = pl.BlockSpec(memory_space=pl.ANY)
    first, twist, second = const_split(first).swapaxes(0, 1), const(twist), const_split(second)
    room = lambda *arrays: [pltpu.VMEM(array.shape, array.dtype) for array in arrays]
    sems = lambda n: [pltpu.SemaphoreType.DMA((n,)), pltpu.SemaphoreType.DMA((n,))]
    mib = 1024 * 1024
    remote = lambda k, limit: pltpu.CompilerParams(vmem_limit_bytes=limit, collective_id=k, has_side_effects=True)
    alpha, mix = const(alpha), const_split(mix)
    swap = jnp.asarray(swap.astype(np.float32).astype(bf16))
    table = pl.pallas_call(
        lambda *refs: transform_kernel(size_x, size_y, own, half, total, *refs),
        out_shape=jax.ShapeDtypeStruct((rows // 16, 128), f32),
        in_specs=[hbm] * 7,
        out_specs=vmem,
        scratch_shapes=[
            pltpu.VMEM((count * half * 2, 128), f32),
            pltpu.VMEM(turned.shape, f32),
            pltpu.VMEM((RAD, own * RAD), bf16),
            pltpu.VMEM((RAD, own * RAD), bf16),
            pltpu.VMEM((count * half * 2, 128), f32),
            pltpu.VMEM((2, count, 128), f32),
        ] + room(first, twist, second, alpha, mix, swap) + sems(2) + [pltpu.SemaphoreType.DMA((7,))],
        compiler_params=remote(0, 60 * mib),
        name="transform",
    )(turned, first, twist, second, alpha, mix, swap)
    table = table.reshape(rows // 128, 8, 128)

    all_residue = (base * np.array([1, -1])[None, :, None]) % RAD
    lane = np.arange(VL)
    back = np.stack([lane, VL - 1 - lane])
    place = back[None, :, None, :] * RAD + all_residue[..., None]
    place = jnp.asarray(np.tile(place.reshape(RAD, VL), (1, 2)).astype(np.int32))
    angle = np.stack([grid(back[0], lane, VL), grid(back[1], lane, VL)])
    both = np.stack([np.cos(angle), -np.sin(angle)])
    inner = const_split(np.einsum("bd,chvt->bvhcdt", np.eye(2), both).reshape(2 * VL, 8 * VL))
    angle = np.tile(grid(all_residue.reshape(-1), lane, BL), (1, 2))
    spin = const(np.stack([np.cos(angle), np.sin(angle)]))
    angle = grid(span, all_residue.reshape(-1), RAD)
    cos_m, sin_m = np.cos(angle), np.sin(angle)
    outer = const_split(np.block([[cos_m, sin_m], [-sin_m, cos_m]]))
    when = jnp.asarray(np.tile(np.arange(BL).reshape(RAD, VL), (1, 2)).astype(np.int32))
    return pl.pallas_call(
        lambda *refs: deliver_kernel(size_x, size_y, half, total, *refs),
        out_shape=jax.ShapeDtypeStruct((pairs, RAD, 128), f32),
        in_specs=[smem] * 4 + [hbm] * 6,
        out_specs=vmem,
        scratch_shapes=[
            pltpu.VMEM(shape, f32),
            pltpu.VMEM(shape, f32),
            pltpu.VMEM((pairs, RAD, 128), f32),
            pltpu.VMEM((pairs, 2, RAD, 128), f32),
        ] + room(place, inner, spin, outer, when, table) + sems(1) + [pltpu.SemaphoreType.DMA((6,))],
        compiler_params=remote(1, 48 * mib),
        name="deliver",
    )(*bands, table, place, inner, spin, outer, when)


def body(signal, band_start, band_width, band_gain, slot_band):
    devices = lax.axis_size("tx") * lax.axis_size("ty")
    length = signal.shape[0]
    total = length * devices
    own = length // (RAD * RAD)
    cols = own * devices
    chunk = length // cols
    base = row_bases(devices)
    half = base.shape[2]

    turned = signal.reshape(chunk // RAD, RAD, cols).transpose(2, 0, 1)
    turned = turned.reshape(devices, own, chunk // RAD, RAD)
    slots = slot_band.shape[0] // devices
    result = spectrum(turned, (band_start, band_width, band_gain, slot_band), base, total)
    result = result.reshape(slots // 2, RAD, 2, VL).transpose(0, 2, 1, 3)
    return result.reshape(slots, BL)


def solution(mesh):
    return jax.shard_map(
        body,
        mesh=mesh,
        in_specs=(P(AXES), P(), P(), P(), P()),
        out_specs=P(AXES, None),
        check_vma=False,
    )
```

```python
import math

import jax
import jax.numpy as jnp
import numpy as np
from jax import lax
from jax.experimental import pallas as pl
from jax.experimental.pallas import tpu as pltpu
from jax.sharding import PartitionSpec as P

BL = 16384
RAD = 256
VL = BL // RAD

two_pi = 2.0 * math.pi
AXES = ("tx", "ty")


def grid(first, second, modulus):
    return (two_pi / modulus) * (np.outer(first, second) % modulus)


def const(array):
    return jnp.asarray(np.ascontiguousarray(array, dtype=np.float32))


def row_bases(devices):
    half = RAD // (2 * devices)
    base = np.zeros((devices, 2, half), np.int64)
    for f in range(devices):
        for i in range(half):
            base[f, :, i] = f + 2 * devices * i if f else devices * i
    base[0, 1, 0] = RAD // 2
    return base


def split(array):
    high = array.astype(jnp.bfloat16)
    return high, (array - high.astype(jnp.float32)).astype(jnp.bfloat16)


def const_split(array):
    array = np.ascontiguousarray(array, dtype=np.float32)
    high = array.astype(jnp.bfloat16)
    return jnp.asarray(np.stack([high, (array - high.astype(np.float32)).astype(jnp.bfloat16)]))


def product(left, right):
    (left_high, left_low), (right_high, right_low) = left, right
    one = lambda a, b: jnp.dot(a, b, preferred_element_type=jnp.float32)
    return one(left_high, right_high) + (one(left_high, right_low) + one(left_low, right_high))


def meet(size_x, size_y, send_sem, recv_sem):
    devices = size_x * size_y
    me = lax.axis_index("tx") * size_y + lax.axis_index("ty")
    barrier = pltpu.get_barrier_semaphore()

    def greet(j, carry):
        to = lax.rem(me + j, devices)
        pl.semaphore_signal(
            barrier, inc=1, device_id=(to // size_y, lax.rem(to, size_y)), device_id_type=pl.DeviceIdType.MESH
        )
        return carry

    lax.fori_loop(1, devices, greet, 0)
    pl.semaphore_wait(barrier, devices - 1)

    def send(stage, source, target, to):
        pltpu.make_async_remote_copy(
            src_ref=source, dst_ref=target, send_sem=send_sem.at[stage], recv_sem=recv_sem.at[stage],
            device_id=(to // size_y, lax.rem(to, size_y)), device_id_type=pl.DeviceIdType.MESH,
        ).start()

    def wait(ref, sem):
        pltpu.make_async_copy(ref, ref, sem).wait()

    return devices, me, send, wait


def fetch(sem, *pairs):
    loads = [pltpu.make_async_copy(source, target, sem.at[k]) for k, (source, target) in enumerate(pairs)]
    for load in loads:
        load.start()
    return loads


def transform_kernel(
    size_x, size_y, own, half, total,
    turned_ref, first_hbm, twist_hbm, second_hbm, alpha_hbm, mix_hbm, swap_hbm,
    table_ref, value_ref, column_ref, high_ref, low_ref, pass_ref, beta_ref,
    first_ref, twist_ref, second_ref, alpha_ref, mix_ref, swap_ref,
    send_sem, recv_sem, load_sem,
):
    devices, me, send, wait = meet(size_x, size_y, send_sem, recv_sem)
    others = devices - 1
    high_rows = 2 * own
    span = 2 * half * high_rows

    def send_columns(j, carry):
        to = lax.rem(me + j, devices)
        send(0, turned_ref.at[to], column_ref.at[me], to)
        return carry

    lax.fori_loop(1, devices, send_columns, 0)
    loads = fetch(
        load_sem, (turned_ref.at[me], column_ref.at[me]),
        (first_hbm, first_ref), (twist_hbm, twist_ref), (second_hbm, second_ref),
        (alpha_hbm, alpha_ref), (mix_hbm, mix_ref), (swap_hbm, swap_ref),
    )
    for load in loads:
        load.wait()
    wait(column_ref.at[pl.ds(0, others)], recv_sem.at[0])
    for c in range(own):
        high, low = split(column_ref[:, c].reshape(RAD, RAD))
        high_ref[:, c * RAD : (c + 1) * RAD] = high
        low_ref[:, c * RAD : (c + 1) * RAD] = low

    group = first_ref.shape[0]
    height = half * 8

    def transform(b, carry):
        at = lax.rem(b + me // 8, group)
        section = product((first_ref[at, 0], first_ref[at, 1]), (high_ref[...], low_ref[...]))
        twist_cos, twist_sin = twist_ref[at, 0], twist_ref[at, 1]
        turned = []
        for c in range(own):
            real = section[: 2 * height, c * RAD : (c + 1) * RAD]
            imag = section[2 * height :, c * RAD : (c + 1) * RAD]
            turned.append(
                jnp.concatenate([real * twist_cos + imag * twist_sin, imag * twist_cos - real * twist_sin], axis=1)
            )
        for h in range(2):
            left = jnp.concatenate([part[h * height : (h + 1) * height] for part in turned], axis=0)
            bins = product(split(left), (second_ref[0, h], second_ref[1, h]))
            for c in range(own):
                for i in range(half):
                    row = c * height + i * 8
                    for side in range(2):
                        tile = (2 * i + side) * high_rows
                        pass_ref[pl.ds(at * 8 * span + tile + h * own + c, 8, stride=span), :] = bins[
                            row : row + 8, side * 128 : side * 128 + 128
                        ]
        for j in range(8):
            to = at * 8 + lax.rem(me + j, 8)

            @pl.when(to != me)
            def _():
                part = lambda ref, k: ref.at[pl.ds(pl.multiple_of(k * span, span), span)]
                send(1, part(pass_ref, to), part(value_ref, me), to)

        return carry

    lax.fori_loop(0, group, transform, 0)
    mine = pl.ds(pl.multiple_of(me * span, span), span)
    value_ref[mine, :] = pass_ref[mine, :]

    count = alpha_ref.shape[1]
    cols = count // 2
    row = lax.broadcasted_iota(jnp.int32, (count, 128), 0)
    lane = lax.broadcasted_iota(jnp.int32, (count, 128), 1)
    at = jnp.where(me == 0, jnp.where(lane == half, RAD // 2, devices * lane), me + 2 * devices * lane)
    angle = (row // high_rows * own + row % own) * at
    angle = angle.astype(jnp.float32) * (two_pi / total)
    beta_ref[0] = jnp.cos(angle)
    beta_ref[1] = jnp.where(row // own % 2 == 1, -1.0, 1.0) * jnp.sin(angle)
    wait(value_ref.at[pl.ds(0, others * span)], recv_sem.at[1])

    is_upper = lax.broadcasted_iota(jnp.int32, (count, RAD), 0) // own % 2 == 1

    def exchange_rows(block):
        cut = block.reshape(count // (2 * own), 2, own, RAD)
        return jnp.concatenate([cut[:, 1:], cut[:, :1]], axis=1).reshape(count, RAD)

    def twist(block, at):
        beta_cos, beta_sin = beta_ref[0, :, at : at + 1], beta_ref[1, :, at : at + 1]
        theta_cos = alpha_ref[0] * beta_cos - alpha_ref[1] * beta_sin
        theta_sin = alpha_ref[1] * beta_cos + alpha_ref[0] * beta_sin
        return theta_cos * block + theta_sin * exchange_rows(block)

    mix = mix_ref[0], mix_ref[1]

    def values(i):
        part = value_ref[...].reshape(devices, 2 * half, high_rows, 128)
        return jnp.concatenate([part[:, 2 * i + side].reshape(count, 128) for side in range(2)], axis=1)

    def put(result, h, i):
        for side in range(2):
            at = pl.ds(8 * side + h * half + i, cols, stride=16)
            table_ref.reshape(total // RAD // 16, 128)[at, :] = result[:, side * 128 : (side + 1) * 128]

    def general(i):
        result = product(mix, split(twist(values(i), i)))
        for h in range(2):
            put(result[h * cols : (h + 1) * cols], h, i)

    for i in range(1, half):
        general(i)

    @pl.when(me != 0)
    def _():
        general(0)

    @pl.when(me == 0)
    def _():
        block = values(0)
        high, low = split(block)
        for h in range(2):
            turn = lambda part: jnp.dot(part, swap_ref[h], preferred_element_type=jnp.float32)
            mirror = exchange_rows(turn(high) + turn(low))
            keep = is_upper if h else ~is_upper
            spun = split(twist(jnp.where(keep, block, mirror), h * half))
            rows_of = slice(h * cols, (h + 1) * cols)
            put(product((mix_ref[0, rows_of], mix_ref[1, rows_of]), spun), h, 0)

    wait(turned_ref.at[pl.ds(0, others)], send_sem.at[0])
    wait(pass_ref.at[pl.ds(0, others * span)], send_sem.at[1])
    return devices, me, send, wait


def deliver_kernel(
    shared, half, total,
    start_ref, width_ref, gains_ref, slot_ref, table_ref, place_hbm, inner_hbm, twist_hbm, outer_hbm, when_hbm,
    out_ref, leave_ref, land_ref, gain_ref, phase_ref, place_ref, inner_ref, twist_ref, outer_ref, when_ref,
    send_sem, recv_sem, load_sem,
):
    loads = fetch(
        load_sem, (place_hbm, place_ref), (when_hbm, when_ref), (inner_hbm, inner_ref), (twist_hbm, twist_ref),
        (outer_hbm, outer_ref),
    )
    devices, me, send, wait = shared
    pairs, height = leave_ref.shape[1:3]
    rows = total // RAD
    shape = (2 * half, 128)
    lane = lax.broadcasted_iota(jnp.int32, shape, 1)
    is_low = lane < VL
    is_back = lax.broadcasted_iota(jnp.int32, shape, 0) >= half
    row = lax.broadcasted_iota(jnp.int32, shape, 0)
    index = jnp.where(is_back, row - half, row)
    residue = jnp.where(me == 0, devices * index, me + 2 * devices * index)
    residue = jnp.where((me == 0) & (row == half), RAD // 2, residue)
    residue = jnp.where(is_back, RAD - residue, residue)

    def load(tile):
        return table_ref[tile][: 2 * half]

    def window(slot):
        start = start_ref[jnp.maximum(slot_ref[slot], 0)]
        block = start // BL
        back = rows // VL - 2 - block
        tiles_of = [block // 2, (block + 1) // 2, back // 2, (back + 1) // 2]
        ahead_high, ahead_low, back_high, back_low = [load(t) for t in tiles_of]
        picked = jnp.where(is_low, jnp.where(is_back, back_low, ahead_low), jnp.where(is_back, back_high, ahead_high))
        ahead_at = 128 * jnp.where(is_low, tiles_of[1], tiles_of[0]) + lane
        back_at = rows - 1 - (128 * jnp.where(is_low, tiles_of[3], tiles_of[2]) + lane)
        place = RAD * jnp.where(is_back, back_at, ahead_at) + residue - start
        picked = jnp.where((place >= 0) & (place < BL), picked, 0.0)
        return picked + pltpu.roll(picked, VL, 1)

    def step(j, carry):
        to = lax.rem(me + j, devices)
        for k in range(pairs):
            slot = 2 * (to * pairs + k)
            leave_ref[to, k] = jnp.where(is_low, window(slot), window(slot + 1))

        @pl.when(to != me)
        def _():
            send(2, leave_ref.at[to], land_ref.at[me], to)

        return carry

    lax.fori_loop(1, devices + 1, step, 0)
    land_ref[me] = leave_ref[me]
    for copy in loads:
        copy.wait()

    is_low = lax.broadcasted_iota(jnp.int32, (1, 128), 1) < VL
    for p in range(pairs):
        slots = [slot_ref[(me * pairs + p) * 2 + k] for k in range(2)]
        of = lambda ref: jnp.where(is_low, *[ref[jnp.maximum(slot, 0)] for slot in slots])
        shift = of(start_ref) & (BL - 1)
        width = of(width_ref)
        rate = two_pi / width.astype(jnp.float32)
        scale = jnp.where(jnp.where(is_low, *slots) >= 0, of(gains_ref) / jnp.sqrt(width.astype(jnp.float32)), 0.0)
        position = (place_ref[...] - shift) & (BL - 1)
        turn = (position.astype(jnp.float32) + 0.5) * rate
        gain_ref[p] = jnp.where(position < width, 0.5 - 0.5 * jnp.cos(turn), 0.0)
        angle = ((when_ref[...] * shift) & (BL - 1)).astype(jnp.float32) * (two_pi / BL)
        phase_cos, phase_sin = jnp.cos(angle), jnp.sin(angle)
        phase_ref[p, 0] = (phase_cos - phase_sin) * scale
        phase_ref[p, 1] = (phase_cos + phase_sin) * scale

    wait(land_ref.at[pl.ds(0, devices - 1)], recv_sem.at[2])
    is_back = lax.broadcasted_iota(jnp.int32, (RAD, 1), 0) % height >= height // 2
    stacked = []
    for p in range(pairs):
        tapered = land_ref[:, p].reshape(RAD, 128) * gain_ref[p]
        part = product(split(tapered), (inner_ref[0], inner_ref[1]))
        part = jnp.where(is_back, part[:, 256:], part[:, :256])
        real, imag = part[:, :128], part[:, 128:]
        twist_cos, twist_sin = twist_ref[0], twist_ref[1]
        stacked.append(
            jnp.concatenate([real * twist_cos + imag * twist_sin, imag * twist_cos - real * twist_sin], axis=0)
        )
    result = product((outer_ref[0], outer_ref[1]), split(jnp.concatenate(stacked, axis=1)))
    for p in range(pairs):
        lanes = slice(p * 128, (p + 1) * 128)
        out_ref[p] = result[:RAD, lanes] * phase_ref[p, 0] - result[RAD:, lanes] * phase_ref[p, 1]
    wait(leave_ref.at[pl.ds(0, devices - 1)], send_sem.at[2])


def spectrum_kernel(size_x, size_y, own, half, total, *refs):
    bands, first, last, out_ref = refs[:4], refs[4:11], refs[11:16], refs[16]
    scratch, rest, sems = refs[17:30], refs[30:39], refs[39:]
    shared = transform_kernel(size_x, size_y, own, half, total, *first, *scratch, *sems[:3])
    deliver_kernel(shared, half, total, *bands, scratch[0], *last, out_ref, *rest, *sems[:2], sems[3])


def spectrum(turned, bands, base, total):
    size_x, size_y = lax.axis_size("tx"), lax.axis_size("ty")
    devices, _, half = base.shape
    own = turned.shape[1]
    cols = devices * own
    count = 2 * cols
    span = np.arange(RAD)
    col = np.arange(cols)
    sign = np.array([1.0, -1.0])[None, :, None]

    def rows_of(angle):
        part = angle.reshape(devices, 1, own, -1)
        put = lambda array: np.broadcast_to(array, (devices, 2, own, part.shape[-1])).reshape(count, -1)
        return np.stack([put(np.cos(part)), put(sign[..., None] * np.sin(part))]).astype(np.float32)

    alpha = rows_of(grid(col, RAD * span, total))
    angle = grid(col, col, cols).reshape(cols, devices, 1, own)
    ahead = np.concatenate([np.cos(angle), np.sin(angle)], axis=2)
    back = np.concatenate([-np.sin(angle), np.cos(angle)], axis=2)
    mix = np.stack([ahead, back]).reshape(count, count)
    swap = np.zeros((2, RAD, RAD))
    swap[0, (-span) % RAD, span] = 1.0
    swap[1, RAD - 1 - span, span] = 1.0
    order = base.reshape(devices // 8, 8, 2, half).transpose(0, 2, 3, 1).reshape(devices // 8, -1)
    angle = grid(order.reshape(-1), span, RAD).reshape(order.shape + (RAD,))
    first = np.concatenate([np.cos(angle), -np.sin(angle)], axis=1)
    angle = grid(order.reshape(-1), span, RAD * RAD).reshape(order.shape + (RAD,))
    twist = np.stack([np.cos(angle), np.sin(angle)], axis=1)
    angle = grid(span, span, RAD)
    cos_m, sin_m = np.cos(angle), np.sin(angle)
    minus = np.concatenate([cos_m + sin_m, sin_m - cos_m], axis=0)
    plus = np.concatenate([cos_m - sin_m, cos_m + sin_m], axis=0)
    second = np.stack([minus, plus]) / math.sqrt(total)
    smem = pl.BlockSpec(memory_space=pltpu.SMEM)
    vmem = pl.BlockSpec(memory_space=pltpu.VMEM)
    rows = total // RAD
    pairs = bands[3].shape[0] // (2 * devices)
    shape = (devices, pairs, 2 * half, 128)
    f32, bf16 = jnp.float32, jnp.bfloat16
    hbm = pl.BlockSpec(memory_space=pl.ANY)
    first, twist, second = const_split(first).swapaxes(0, 1), const(twist), const_split(second)
    room = lambda *arrays: [pltpu.VMEM(array.shape, array.dtype) for array in arrays]
    alpha, mix = const(alpha), const_split(mix)
    swap = jnp.asarray(swap.astype(np.float32).astype(bf16))

    all_residue = (base * np.array([1, -1])[None, :, None]) % RAD
    lane = np.arange(VL)
    back = np.stack([lane, VL - 1 - lane])
    place = back[None, :, None, :] * RAD + all_residue[..., None]
    place = jnp.asarray(np.tile(place.reshape(RAD, VL), (1, 2)).astype(np.int32))
    angle = np.stack([grid(back[0], lane, VL), grid(back[1], lane, VL)])
    both = np.stack([np.cos(angle), -np.sin(angle)])
    inner = const_split(np.einsum("bd,chvt->bvhcdt", np.eye(2), both).reshape(2 * VL, 8 * VL))
    angle = np.tile(grid(all_residue.reshape(-1), lane, BL), (1, 2))
    spin = const(np.stack([np.cos(angle), np.sin(angle)]))
    angle = grid(span, all_residue.reshape(-1), RAD)
    cos_m, sin_m = np.cos(angle), np.sin(angle)
    outer = const_split(np.block([[cos_m, sin_m], [-sin_m, cos_m]]))
    when = jnp.asarray(np.tile(np.arange(BL).reshape(RAD, VL), (1, 2)).astype(np.int32))
    dma = lambda n: pltpu.SemaphoreType.DMA((n,))
    scratch = [
        pltpu.VMEM((rows // 128, 8, 128), f32),
        pltpu.VMEM((count * half * 2, 128), f32),
        pltpu.VMEM(turned.shape, f32),
        pltpu.VMEM((RAD, own * RAD), bf16),
        pltpu.VMEM((RAD, own * RAD), bf16),
        pltpu.VMEM((count * half * 2, 128), f32),
        pltpu.VMEM((2, count, 128), f32),
    ] + room(first, twist, second, alpha, mix, swap)
    rest = [
        pltpu.VMEM(shape, f32),
        pltpu.VMEM(shape, f32),
        pltpu.VMEM((pairs, RAD, 128), f32),
        pltpu.VMEM((pairs, 2, RAD, 128), f32),
    ] + room(place, inner, spin, outer, when)
    return pl.pallas_call(
        lambda *refs: spectrum_kernel(size_x, size_y, own, half, total, *refs),
        out_shape=jax.ShapeDtypeStruct((pairs, RAD, 128), f32),
        in_specs=[smem] * 4 + [hbm] * 12,
        out_specs=vmem,
        scratch_shapes=scratch + rest + [dma(3), dma(3), dma(6 + 1), dma(5)],
        compiler_params=pltpu.CompilerParams(
            vmem_limit_bytes=60 * 1024 * 1024, collective_id=0, has_side_effects=True
        ),
        name="spectrum",
    )(*bands, turned, first, twist, second, alpha, mix, swap, place, inner, spin, outer, when)


def body(signal, band_start, band_width, band_gain, slot_band):
    devices = lax.axis_size("tx") * lax.axis_size("ty")
    length = signal.shape[0]
    total = length * devices
    own = length // (RAD * RAD)
    cols = own * devices
    chunk = length // cols
    base = row_bases(devices)
    half = base.shape[2]

    turned = signal.reshape(chunk // RAD, RAD, cols).transpose(2, 0, 1)
    turned = turned.reshape(devices, own, chunk // RAD, RAD)
    slots = slot_band.shape[0] // devices
    result = spectrum(turned, (band_start, band_width, band_gain, slot_band), base, total)
    result = result.reshape(slots // 2, RAD, 2, VL).transpose(0, 2, 1, 3)
    return result.reshape(slots, BL)


def solution(mesh):
    return jax.shard_map(
        body,
        mesh=mesh,
        in_specs=(P(AXES), P(), P(), P(), P()),
        out_specs=P(AXES, None),
        check_vma=False,
    )
```
